768 devices in a mesh: row: 32 (over z_lo, x, core), col: 24 (over y, z_hi).
Axes of the slice: x: 4, y: 8, z: 12 (z_hi: 3, z_lo: 4; z = z_hi * 4 + z_lo), core: 2. Of those that a mesh axis runs over, the one named last changes fastest.
Arguments:
- node_latents: bfloat16 [24576, 512], P(('row', 'col')), may hold values from -6 to 6
- edge_latents: bfloat16 [196608, 512], P(('row', 'col')), may hold values from -6 to 6
- edge_sender: int32 [196608], P(('row', 'col')), may hold values from 0 to 767
- edge_receiver: int32 [196608], P(('row', 'col')), may hold values from 0 to 1023, as said below
- edge_count: int32 [768, 32], P(('row', 'col')), may hold values from 1 to 8, as said below
- w_in: bfloat16 [1536, 512], replicated, may hold values from -0.15625 to 0.15625
- b_in: float32 [512], replicated, may hold values from -4 to 4
- w_out: bfloat16 [512, 512], replicated, may hold values from -0.25 to 0.25
- b_out: float32 [512], replicated, may hold values from -4 to 4
- ln_gain: float32 [512], replicated, may hold values from 0.5 to 1.5
- ln_bias: float32 [512], replicated, may hold values from -3 to 3
- agg_cotangent: bfloat16 [24576, 512], P(('row', 'col')), may hold values from -6 to 6
- edge_cotangent: bfloat16 [196608, 512], P(('row', 'col')), may hold values from -6 to 6
Outputs:
- new_edges: bfloat16 [196608, 512], P(('row', 'col'))
- aggregated: bfloat16 [24576, 512], P(('row', 'col'))
- grad_nodes: bfloat16 [24576, 512], P(('row', 'col'))
- grad_edges: bfloat16 [196608, 512], P(('row', 'col'))
The draws below stay inside these ranges and needn't reach their ends.
Inputs may be any that keep to these rules, and one draw needn't show every extreme that they name: `edge_receiver`: on every device, slots of receiver block b name receivers in b * 32 to (b + 1) * 32 - 1, non-decreasing within the block. `edge_count`: every device has a receiver block with exactly 8 live slots.
All inputs are finite; a program needn't handle non-finite values.
Results may differ from the reference program's by a relative error of at most 0.009.
Values may be sent and summed in bfloat16 or wider, within the bound.
No kernel may reach another device: no remote copies, remote signals or barrier semaphores. Data moves between devices by JAX's collectives and lax.ppermute only.
A program may use at most 32 MiB of HBM per device.

```python
import jax
import jax.numpy as jnp
from jax import lax

D = 512
FF = 512
NODE_DEV = 32
EDGE_DEV = 256
SLOT = 8
TILES = 768
NODES = 24576
EDGES = 196608
N_COL = 24


def draw_edge_receiver(key, part):
    key = jax.random.fold_in(key, 11)
    blocks = EDGE_DEV // SLOT
    values = jax.random.randint(key, (TILES, blocks, SLOT), 0, NODE_DEV)
    column = jnp.arange(SLOT)[None, None, :]
    values = jnp.where(column == 0, 0, jnp.where(column == SLOT - 1, NODE_DEV - 1, values))
    values = jnp.sort(values, axis=-1)
    values = values + (jnp.arange(blocks) * NODE_DEV)[None, :, None]
    return values.reshape(EDGES).astype(jnp.int32)


def draw_edge_count(key, part):
    key = jax.random.fold_in(key, 23)
    first, second = jax.random.split(key)
    blocks = EDGE_DEV // SLOT
    lowest = max(1, SLOT // 4)
    values = jax.random.randint(first, (TILES, blocks), lowest, SLOT + 1)
    chosen = jax.random.randint(second, (TILES, 1), 0, blocks)
    values = jnp.where(jnp.arange(blocks)[None, :] == chosen, SLOT, values)
    return values.astype(jnp.int32)


def plant(result, own_key, least, top_value):
    longest = result.shape.index(max(result.shape))
    spots = []
    for shift in (0, 1):
        where = [jax.random.randint(jax.random.fold_in(own_key, axis), (), 0, length) for axis, length in enumerate(result.shape)]
        where[longest] = (where[longest] + shift) % result.shape[longest]
        spots.append(tuple(where))
    return result.at[spots[0]].set(least).at[spots[1]].set(top_value)


def steps_of(key, extent, shards, least, top_value):
    def one(position, shards_of):
        heights = jax.random.uniform(jax.random.fold_in(jax.random.fold_in(key, 6), position), (shards_of,), jnp.float32, least / len(shards), top_value / len(shards))
        return jnp.repeat(jnp.exp(heights), extent[position] // shards_of).reshape((-1,) + (1,) * (len(extent) - position - 1))

    factor_of = one(*shards[0])
    for cut in shards[1:]:
        factor_of = factor_of * one(*cut)
    return factor_of


def gaussian(own_key, dims, scale, reach, cuts=(), kind=jnp.bfloat16):
    drawn = scale * jax.random.normal(own_key, dims, jnp.float32)
    if cuts:
        drawn = drawn * steps_of(own_key, dims, cuts, -0.22, 0.18)
    return jnp.clip(drawn, -reach, reach).astype(kind)


def setup_inputs(seed: int = 0) -> dict:
    arg_keys = jax.random.split(jax.random.key(seed), 14)
    node_latents = gaussian(arg_keys[0], (NODES, D), 1.0, 6.0, ((0, 768),))
    edge_latents = gaussian(arg_keys[1], (EDGES, D), 1.0, 6.0, ((0, 768),))
    edge_sender = plant(jax.random.randint(arg_keys[2], (EDGES,), 0, N_COL * NODE_DEV), jax.random.fold_in(arg_keys[2], 1), 0, (N_COL * NODE_DEV) - 1).astype(jnp.int32)
    edge_receiver = draw_edge_receiver(jax.random.fold_in(arg_keys[13], 71), 0)
    edge_count = draw_edge_count(jax.random.fold_in(arg_keys[13], 71), 0)
    w_in = gaussian(arg_keys[5], (3 * D, FF), (3 * D) ** -0.5, 0.15625)
    b_in = gaussian(arg_keys[6], (FF,), 1.0, 4.0, (), jnp.float32)
    w_out = gaussian(arg_keys[7], (FF, D), FF ** -0.5, 0.25)
    b_out = gaussian(arg_keys[8], (D,), 1.0, 4.0, (), jnp.float32)
    ln_gain = jnp.clip(1.0 + 0.1 * jax.random.normal(arg_keys[9], (D,), jnp.float32), 0.5, 1.5)
    ln_bias = gaussian(arg_keys[10], (D,), 0.5, 3.0, (), jnp.float32)
    agg_cotangent = gaussian(arg_keys[11], (NODES, D), 1.0, 6.0, ((0, 768),))
    edge_cotangent = gaussian(arg_keys[12], (EDGES, D), 1.0, 6.0, ((0, 768),))
    return dict(node_latents=node_latents, edge_latents=edge_latents, edge_sender=edge_sender, edge_receiver=edge_receiver, edge_count=edge_count, w_in=w_in, b_in=b_in, w_out=w_out, b_out=b_out, ln_gain=ln_gain, ln_bias=ln_bias, agg_cotangent=agg_cotangent, edge_cotangent=edge_cotangent)


def edge_pass(edges, send_feat, recv_feat, live, cotangent, w_in, b_in, w_out, b_out, ln_gain, ln_bias):
    joined = jnp.concatenate([edges, send_feat, recv_feat], axis=1)
    pre_act = jnp.dot(joined, w_in, preferred_element_type=jnp.float32) + b_in
    hidden = jax.nn.silu(pre_act).astype(jnp.bfloat16)
    outer = jnp.dot(hidden, w_out, preferred_element_type=jnp.float32) + b_out
    center = outer - lax.optimization_barrier(jnp.mean(outer, axis=1, keepdims=True))
    inv_std = lax.rsqrt(lax.optimization_barrier(jnp.mean(center * center, axis=1, keepdims=True)) + 1e-05)
    normed = center * inv_std
    message = jnp.where(live[:, None], normed * ln_gain + ln_bias, 0.0).astype(jnp.bfloat16)
    new_edges = (edges.astype(jnp.float32) + message.astype(jnp.float32)).astype(jnp.bfloat16)
    cot = jnp.where(live[:, None], cotangent, 0.0)
    scaled = cot * ln_gain
    d_outer = inv_std * (scaled - lax.optimization_barrier(jnp.mean(scaled, axis=1, keepdims=True)) - normed * lax.optimization_barrier(jnp.mean(scaled * normed, axis=1, keepdims=True)))
    d_outer = d_outer.astype(jnp.bfloat16)
    d_hidden = lax.dot_general(d_outer, w_out, (((1,), (1,)), ((), ())), preferred_element_type=jnp.float32)
    sigma = jax.nn.sigmoid(pre_act)
    d_pre = (d_hidden * sigma * (1.0 + pre_act * (1.0 - sigma))).astype(jnp.bfloat16)
    d_in = lax.dot_general(d_pre, w_in, (((1,), (1,)), ((), ())), preferred_element_type=jnp.float32)
    width = edges.shape[1]
    d_edge = d_in[:, :width]
    d_send = d_in[:, width:2 * width].astype(jnp.bfloat16)
    d_recv = d_in[:, 2 * width:].astype(jnp.bfloat16)
    return (message, new_edges, d_edge, d_send, d_recv)

def reference(node_latents, edge_latents, edge_sender, edge_receiver, edge_count, w_in, b_in, w_out, b_out, ln_gain, ln_bias, agg_cotangent, edge_cotangent):
    slot_ids = jnp.arange(EDGES).astype(jnp.int32)
    tile = slot_ids // EDGE_DEV
    tile_row = tile // N_COL
    tile_col = tile % N_COL
    inside = slot_ids % EDGE_DEV
    block = inside // SLOT
    live = inside % SLOT < edge_count[tile, block]
    sender_node = ((tile_row * N_COL + edge_sender // NODE_DEV) * NODE_DEV + edge_sender % NODE_DEV).astype(jnp.int32)
    receiver_node = ((edge_receiver // NODE_DEV * N_COL + tile_col) * NODE_DEV + edge_receiver % NODE_DEV).astype(jnp.int32)

    def one_tile(args):
        edges, send_idx, recv_idx, live_t, edge_cot = args
        send_feat = node_latents[send_idx]
        recv_feat = node_latents[recv_idx]
        cotangent = edge_cot.astype(jnp.float32) + agg_cotangent[recv_idx].astype(jnp.float32)
        message, new_edges, d_edge, d_send, d_recv = edge_pass(edges, send_feat, recv_feat, live_t, cotangent, w_in, b_in, w_out, b_out, ln_gain, ln_bias)
        grad_edges = (edge_cot.astype(jnp.float32) + d_edge).astype(jnp.bfloat16)
        return (message, new_edges, grad_edges, d_send, d_recv)
    width = edge_latents.shape[1]
    message, new_edges, grad_edges, d_send, d_recv = lax.map(one_tile, (edge_latents.reshape(TILES, EDGE_DEV, width), sender_node.reshape(TILES, EDGE_DEV), receiver_node.reshape(TILES, EDGE_DEV), live.reshape(TILES, EDGE_DEV), edge_cotangent.reshape(TILES, EDGE_DEV, width)))
    message = message.reshape(EDGES, width).astype(jnp.float32)
    aggregated = jax.ops.segment_sum(message, receiver_node, num_segments=NODES).astype(jnp.bfloat16)
    grad_nodes = jax.ops.segment_sum(d_send.reshape(EDGES, width).astype(jnp.float32), sender_node, num_segments=NODES)
    grad_nodes = grad_nodes + jax.ops.segment_sum(d_recv.reshape(EDGES, width).astype(jnp.float32), receiver_node, num_segments=NODES)
    return (new_edges.reshape(EDGES, width), aggregated, grad_nodes.astype(jnp.bfloat16), grad_edges.reshape(EDGES, width))
```

```python
import functools

import jax
import jax.numpy as jnp
from jax import lax
from jax.experimental import pallas as pl
from jax.experimental.pallas import tpu as pltpu
from jax.sharding import PartitionSpec as P

Z_HI = 3


def dot(a, b):
    return jnp.dot(a, b, preferred_element_type=jnp.float32)


def dot_t(a, b):
    return lax.dot_general(a, b, (((1,), (1,)), ((), ())), preferred_element_type=jnp.float32)


def edge_kernel(
    edges, table, pick, spread, recv, live, edge_cot,
    w_in, b_in, w_out, b_out, gain, bias,
    new_edges, packed, partial,
):
    slots, width = edges.shape
    group = table.shape[0]
    lane = lax.broadcasted_iota(jnp.int32, (slots, group), 1)
    chosen = jnp.where(pick[...] == lane, 1.0, 0.0).astype(jnp.bfloat16)
    send_feat = dot(chosen, table[...]).astype(jnp.bfloat16)
    pre = dot(edges[...], w_in[:width, :])
    pre += dot(recv[:, :width], w_in[2 * width :, :])
    pre += dot(send_feat, w_in[width : 2 * width, :])
    pre += b_in[...]
    sigma = jax.nn.sigmoid(pre)
    hidden = (pre * sigma).astype(jnp.bfloat16)
    outer = dot(hidden, w_out[...]) + b_out[...]
    center = outer - jnp.mean(outer, axis=1, keepdims=True)
    inv_std = lax.rsqrt(jnp.mean(center * center, axis=1, keepdims=True) + 1e-05)
    normed = center * inv_std
    alive = live[...] > 0
    message = jnp.where(alive, normed * gain[...] + bias[...], 0.0).astype(jnp.bfloat16)
    packed[:, :width] = message
    new_edges[...] = (edges[...].astype(jnp.float32) + message.astype(jnp.float32)).astype(jnp.bfloat16)
    cot = edge_cot[...].astype(jnp.float32) + recv[:, width:].astype(jnp.float32)
    scaled = jnp.where(alive, cot, 0.0) * gain[...]
    d_outer = inv_std * (
        scaled
        - jnp.mean(scaled, axis=1, keepdims=True)
        - normed * jnp.mean(scaled * normed, axis=1, keepdims=True)
    )
    d_hidden = dot_t(d_outer.astype(jnp.bfloat16), w_out[...])
    d_pre = (d_hidden * sigma * (1.0 + pre * (1.0 - sigma))).astype(jnp.bfloat16)
    packed[:, width:] = d_pre
    row = lax.broadcasted_iota(jnp.int32, (group, slots), 0)
    placed = jnp.where(spread[...] == row, 1.0, 0.0).astype(jnp.bfloat16)
    partial[...] = dot(placed, d_pre).astype(jnp.bfloat16)


def on_device(
    node_latents,
    edge_latents,
    edge_sender,
    edge_receiver,
    edge_count,
    w_in,
    b_in,
    w_out,
    b_out,
    ln_gain,
    ln_bias,
    agg_cotangent,
    edge_cotangent,
):
    owned, width = node_latents.shape
    slots = edge_latents.shape[0]
    rows = lax.axis_size("row")
    cols = lax.axis_size("col")
    per_block = slots // rows
    tall = cols // Z_HI
    along_y = [[y * Z_HI + h for y in range(tall)] for h in range(Z_HI)]
    up = [(y * Z_HI + h, y * Z_HI + (h + 1) % Z_HI) for y in range(tall) for h in range(Z_HI)]
    down = [(b, a) for a, b in up]
    my_h = lax.axis_index("col") % Z_HI

    block_of = jnp.arange(slots, dtype=jnp.int32) // per_block
    wanted = (edge_receiver - block_of * owned).reshape(rows, per_block)
    asked = lax.all_to_all(wanted, "row", 0, 0, tiled=True).reshape(slots)
    onehot = (asked[:, None] == jnp.arange(owned, dtype=jnp.int32)[None, :]).astype(jnp.bfloat16)
    own = jnp.concatenate([node_latents, agg_cotangent], axis=1)
    answer = dot(onehot, own).astype(jnp.bfloat16)
    recv = lax.all_to_all(answer, "row", 0, 0, tiled=True)

    from_below = lax.ppermute(node_latents, "col", up)
    from_above = lax.ppermute(node_latents, "col", down)
    column = jnp.concatenate([node_latents, from_below, from_above], axis=0)
    table = lax.all_gather(column, "col", axis=0, tiled=True, axis_index_groups=along_y)

    device = edge_sender // owned
    turn = (my_h - device % Z_HI + Z_HI) % Z_HI
    place = ((device // Z_HI) * Z_HI + turn) * owned + edge_sender % owned
    live = (
        jnp.arange(per_block, dtype=jnp.int32)[None, :] < edge_count[0][:, None]
    ).astype(jnp.int32).reshape(slots, 1)

    vmem = pl.BlockSpec(memory_space=pltpu.VMEM)
    new_edges, packed, partial = pl.pallas_call(
        edge_kernel,
        in_specs=[vmem] * 13,
        out_specs=[vmem] * 3,
        out_shape=[
            jax.ShapeDtypeStruct((slots, width), jnp.bfloat16),
            jax.ShapeDtypeStruct((slots, 2 * width), jnp.bfloat16),
            jax.ShapeDtypeStruct((cols * owned, width), jnp.bfloat16),
        ],
        compiler_params=pltpu.CompilerParams(vmem_limit_bytes=40 * 1024 * 1024),
        cost_estimate=pl.CostEstimate(
            flops=2 * slots * width * (5 * width + 2 * cols * owned),
            bytes_accessed=6 * 1024 * 1024,
            transcendentals=slots * width,
        ),
    )(
        edge_latents, table, place.reshape(slots, 1), place.reshape(1, slots), recv, live,
        edge_cotangent, w_in, b_in.reshape(1, -1), w_out, b_out.reshape(1, -1),
        ln_gain.reshape(1, -1), ln_bias.reshape(1, -1),
    )

    parts = lax.all_to_all(partial, "col", 0, 0, tiled=True, axis_index_groups=along_y)
    column_sum = jnp.sum(parts.reshape(tall, Z_HI * owned, width).astype(jnp.float32), axis=0)
    away = column_sum.astype(jnp.bfloat16)
    to_below = lax.ppermute(away[owned : 2 * owned], "col", down)
    to_above = lax.ppermute(away[2 * owned :], "col", up)

    returned = lax.all_to_all(packed, "row", 0, 0, tiled=True)
    summed = lax.dot_general(
        onehot, returned, (((0,), (0,)), ((), ())), preferred_element_type=jnp.float32
    )
    send_sum = column_sum[:owned] + to_below.astype(jnp.float32) + to_above.astype(jnp.float32)
    grad_nodes = dot_t(summed[:, width:].astype(jnp.bfloat16), w_in[2 * width :]) + dot_t(
        send_sum.astype(jnp.bfloat16), w_in[width : 2 * width]
    )
    d_edge = dot_t(packed[:, width:], w_in[:width])
    grad_edges = (edge_cotangent.astype(jnp.float32) + d_edge).astype(jnp.bfloat16)
    return (
        new_edges,
        summed[:, :width].astype(jnp.bfloat16),
        grad_nodes.astype(jnp.bfloat16),
        grad_edges,
    )


def solution(mesh):
    split = P(("row", "col"), None)
    return jax.shard_map(
        on_device,
        mesh=mesh,
        in_specs=(
            split, split, P(("row", "col")), P(("row", "col")), split,
            P(), P(), P(), P(), P(), P(), split, split,
        ),
        out_specs=(split, split, split, split),
        check_vma=False,
    )
```

```python
import functools

import jax
import jax.numpy as jnp
from jax import lax
from jax.experimental import pallas as pl
from jax.experimental.pallas import tpu as pltpu
from jax.sharding import PartitionSpec as P

Z_HI = 3


def dot(a, b):
    return jnp.dot(a, b, preferred_element_type=jnp.float32)


def dot_t(a, b):
    return lax.dot_general(a, b, (((1,), (1,)), ((), ())), preferred_element_type=jnp.float32)


def onehot_of(asked, owned):
    rows, _, per_block = asked.shape
    spread = jnp.broadcast_to(asked[...], (rows, per_block, per_block)).reshape(rows * per_block, per_block)
    slot = lax.broadcasted_iota(jnp.int32, spread.shape, 0) % per_block
    lane = lax.broadcasted_iota(jnp.int32, spread.shape, 1)
    index = jnp.sum(jnp.where(slot == lane, spread, 0), axis=1, keepdims=True)
    node = lax.broadcasted_iota(jnp.int32, (rows * per_block, owned), 1)
    return jnp.where(index % owned == node, 1.0, 0.0).astype(jnp.bfloat16)


def answer_kernel(asked, nodes, cots, answer):
    owned, width = nodes.shape
    onehot = onehot_of(asked, owned)
    answer[:, :width] = dot(onehot, nodes[...]).astype(jnp.bfloat16)
    answer[:, width:] = dot(onehot, cots[...]).astype(jnp.bfloat16)


def edge_kernel(
    table, spread, recv, counts, w_in, w_out, vectors, edges_hbm, cot_hbm,
    new_edges, packed, partial,
    edges, edge_cot, sems,
):
    slots, width = edges.shape
    group = table.shape[0]
    per_block = slots // counts.shape[1]
    edges_copy = pltpu.make_async_copy(edges_hbm, edges, sems.at[0])
    cot_copy = pltpu.make_async_copy(cot_hbm, edge_cot, sems.at[1])
    edges_copy.start()
    cot_copy.start()
    b_in, b_out = vectors[0:1, :], vectors[1:2, :]
    gain, bias = vectors[2:3, :], vectors[3:4, :]
    diagonal = lax.broadcasted_iota(jnp.int32, (slots, slots), 0) == lax.broadcasted_iota(
        jnp.int32, (slots, slots), 1
    )
    pick = jnp.sum(jnp.where(diagonal, spread[...], 0), axis=1, keepdims=True)
    slot = lax.broadcasted_iota(jnp.int32, (slots, counts.shape[1]), 0)
    block = lax.broadcasted_iota(jnp.int32, (slots, counts.shape[1]), 1)
    count = jnp.sum(jnp.where(slot // per_block == block, counts[...], 0), axis=1, keepdims=True)
    alive = slot[:, :1] % per_block < count
    lane = lax.broadcasted_iota(jnp.int32, (slots, group), 1)
    chosen = jnp.where(pick == lane, 1.0, 0.0).astype(jnp.bfloat16)
    send_feat = dot(chosen, table[...]).astype(jnp.bfloat16)
    pre = dot(recv[:, :width], w_in[2 * width :, :])
    pre += dot(send_feat, w_in[width : 2 * width, :])
    edges_copy.wait()
    pre += dot(edges[...], w_in[:width, :])
    pre += b_in
    sigma = jax.nn.sigmoid(pre)
    hidden = (pre * sigma).astype(jnp.bfloat16)
    outer = dot(hidden, w_out[...]) + b_out
    center = outer - jnp.mean(outer, axis=1, keepdims=True)
    inv_std = lax.rsqrt(jnp.mean(center * center, axis=1, keepdims=True) + 1e-05)
    normed = center * inv_std
    message = jnp.where(alive, normed * gain + bias, 0.0).astype(jnp.bfloat16)
    packed[:, :width] = message
    new_edges[...] = (edges[...].astype(jnp.float32) + message.astype(jnp.float32)).astype(jnp.bfloat16)
    cot_copy.wait()
    cot = edge_cot[...].astype(jnp.float32) + recv[:, width:].astype(jnp.float32)
    scaled = jnp.where(alive, cot, 0.0) * gain
    d_outer = inv_std * (
        scaled
        - jnp.mean(scaled, axis=1, keepdims=True)
        - normed * jnp.mean(scaled * normed, axis=1, keepdims=True)
    )
    d_hidden = dot_t(d_outer.astype(jnp.bfloat16), w_out[...])
    d_pre = (d_hidden * sigma * (1.0 + pre * (1.0 - sigma))).astype(jnp.bfloat16)
    packed[:, width:] = d_pre
    row = lax.broadcasted_iota(jnp.int32, (group, slots), 0)
    placed = jnp.where(spread[...] == row, 1.0, 0.0).astype(jnp.bfloat16)
    partial[...] = dot(placed, d_pre).astype(jnp.bfloat16)


def owner_kernel(asked, returned, column_sum, to_below, to_above, w_back, aggregated, grad_nodes):
    owned, width = aggregated.shape
    onehot = onehot_of(asked, owned)
    summed = lax.dot_general(
        onehot, returned[...], (((0,), (0,)), ((), ())), preferred_element_type=jnp.float32
    )
    aggregated[...] = summed[:, :width].astype(jnp.bfloat16)
    sent = column_sum[...] + to_below[...].astype(jnp.float32) + to_above[...].astype(jnp.float32)
    grad = dot_t(sent.astype(jnp.bfloat16), w_back[:width, :])
    grad += dot_t(summed[:, width:].astype(jnp.bfloat16), w_back[width:, :])
    grad_nodes[...] = grad.astype(jnp.bfloat16)


VMEM = pl.BlockSpec(memory_space=pltpu.VMEM)
ANY = pl.BlockSpec(memory_space=pl.ANY)


def on_device(
    node_latents,
    edge_latents,
    edge_sender,
    edge_receiver,
    edge_count,
    w_in,
    b_in,
    w_out,
    b_out,
    ln_gain,
    ln_bias,
    agg_cotangent,
    edge_cotangent,
):
    owned, width = node_latents.shape
    slots = edge_latents.shape[0]
    rows = lax.axis_size("row")
    cols = lax.axis_size("col")
    per_block = slots // rows
    tall = cols // Z_HI
    along_y = [[y * Z_HI + h for y in range(tall)] for h in range(Z_HI)]
    up = [(y * Z_HI + h, y * Z_HI + (h + 1) % Z_HI) for y in range(tall) for h in range(Z_HI)]
    down = [(b, a) for a, b in up]
    my_h = lax.axis_index("col") % Z_HI

    from_below = lax.ppermute(node_latents, "col", up)
    from_above = lax.ppermute(node_latents, "col", down)
    asked = lax.all_to_all(edge_receiver.reshape(rows, 1, per_block), "row", 0, 0, tiled=True)
    answer = pl.pallas_call(
        answer_kernel,
        in_specs=[VMEM] * 3,
        out_specs=VMEM,
        out_shape=jax.ShapeDtypeStruct((slots, 2 * width), jnp.bfloat16),
        cost_estimate=pl.CostEstimate(
            flops=2 * slots * owned * 2 * width, bytes_accessed=640 * 1024, transcendentals=0
        ),
    )(asked, node_latents, agg_cotangent)
    answer, from_below, from_above = lax.optimization_barrier((answer, from_below, from_above))
    recv = lax.all_to_all(answer, "row", 0, 0, tiled=True)
    column = jnp.concatenate([node_latents, from_below, from_above], axis=0)
    table = lax.all_gather(column, "col", axis=0, tiled=True, axis_index_groups=along_y)

    device = edge_sender // owned
    turn = (my_h - device % Z_HI + Z_HI) % Z_HI
    place = ((device // Z_HI) * Z_HI + turn) * owned + edge_sender % owned
    vectors = jnp.stack([b_in, b_out, ln_gain, ln_bias])

    new_edges, packed, partial = pl.pallas_call(
        edge_kernel,
        in_specs=[VMEM] * 7 + [ANY] * 2,
        out_specs=[VMEM] * 3,
        out_shape=[
            jax.ShapeDtypeStruct((slots, width), jnp.bfloat16),
            jax.ShapeDtypeStruct((slots, 2 * width), jnp.bfloat16),
            jax.ShapeDtypeStruct((cols * owned, width), jnp.bfloat16),
        ],
        scratch_shapes=[
            pltpu.VMEM((slots, width), jnp.bfloat16),
            pltpu.VMEM((slots, width), jnp.bfloat16),
            pltpu.SemaphoreType.DMA((2,)),
        ],
        compiler_params=pltpu.CompilerParams(vmem_limit_bytes=40 * 1024 * 1024),
        cost_estimate=pl.CostEstimate(
            flops=2 * slots * width * (5 * width + 2 * cols * owned),
            bytes_accessed=6 * 1024 * 1024,
            transcendentals=slots * width,
        ),
    )(
        table, place.reshape(1, slots), recv, edge_count, w_in, w_out, vectors,
        edge_latents, edge_cotangent,
    )

    parts = lax.all_to_all(partial, "col", 0, 0, tiled=True, axis_index_groups=along_y)
    column_sum = jnp.sum(parts.reshape(tall, Z_HI * owned, width).astype(jnp.float32), axis=0)
    away = column_sum.astype(jnp.bfloat16)
    to_below = lax.ppermute(away[owned : 2 * owned], "col", down)
    to_above = lax.ppermute(away[2 * owned :], "col", up)

    returned = lax.all_to_all(packed, "row", 0, 0, tiled=True)
    aggregated, grad_nodes = pl.pallas_call(
        owner_kernel,
        in_specs=[VMEM] * 6,
        out_specs=[VMEM] * 2,
        out_shape=[jax.ShapeDtypeStruct((owned, width), jnp.bfloat16)] * 2,
        cost_estimate=pl.CostEstimate(
            flops=2 * owned * width * (2 * slots + 2 * width), bytes_accessed=2 * 1024 * 1024, transcendentals=0
        ),
    )(asked, returned, column_sum[:owned], to_below, to_above, w_in[width:])
    d_edge = dot_t(packed[:, width:], w_in[:width])
    grad_edges = (edge_cotangent.astype(jnp.float32) + d_edge).astype(jnp.bfloat16)
    return (new_edges, aggregated, grad_nodes, grad_edges)


def solution(mesh):
    split = P(("row", "col"), None)
    return jax.shard_map(
        on_device,
        mesh=mesh,
        in_specs=(
            split, split, P(("row", "col")), P(("row", "col")), split,
            P(), P(), P(), P(), P(), P(), split, split,
        ),
        out_specs=(split, split, split, split),
        check_vma=False,
    )
```

```python
import functools

import jax
import jax.numpy as jnp
from jax import lax
from jax.experimental import pallas as pl
from jax.experimental.pallas import tpu as pltpu
from jax.sharding import PartitionSpec as P

Z_HI = 3
Z_LO = 4


def dot(a, b):
    return jnp.dot(a, b, preferred_element_type=jnp.float32)


def dot_t(a, b):
    return lax.dot_general(a, b, (((1,), (1,)), ((), ())), preferred_element_type=jnp.float32)


def column_of(row):
    n = row.shape[1]
    diagonal = lax.broadcasted_iota(jnp.int32, (n, n), 0) == lax.broadcasted_iota(jnp.int32, (n, n), 1)
    return jnp.sum(jnp.where(diagonal, row, 0), axis=1, keepdims=True)


def selector(index, size):
    lane = lax.broadcasted_iota(jnp.int32, (index.shape[0], size), 1)
    return jnp.where(index == lane, 1.0, 0.0).astype(jnp.bfloat16)


def edge_kernel(
    senders, sender, spread, receiver, counts, w_in, w_out, vectors, owners_hbm, edges_hbm, cot_hbm,
    new_edges, packed, partial,
    owners, edges, edge_cot, sems,
):
    slots, width = edges.shape
    group = senders.shape[0]
    blocks = counts.shape[1]
    per_block = slots // blocks
    owned = owners.shape[0] // blocks
    near = blocks // Z_LO
    owners_copy = pltpu.make_async_copy(owners_hbm, owners, sems.at[0])
    edges_copy = pltpu.make_async_copy(edges_hbm, edges, sems.at[1])
    cot_copy = pltpu.make_async_copy(cot_hbm, edge_cot, sems.at[2])
    owners_copy.start()
    edges_copy.start()
    cot_copy.start()
    b_in, b_out = vectors[0:1, :], vectors[1:2, :]
    gain, bias = vectors[2:3, :], vectors[3:4, :]
    slot = lax.broadcasted_iota(jnp.int32, (slots, blocks), 0)
    block = lax.broadcasted_iota(jnp.int32, (slots, blocks), 1)
    count = jnp.sum(jnp.where(slot // per_block == block, counts[...], 0), axis=1, keepdims=True)
    alive = slot[:, :1] % per_block < count
    send_feat = dot(selector(column_of(sender[...]), group), senders[...]).astype(jnp.bfloat16)
    pre = dot(send_feat, w_in[width : 2 * width, :])
    edges_copy.wait()
    pre += dot(edges[...], w_in[:width, :])
    node = column_of(receiver[...])
    owner = node // owned
    where = ((owner % near) * Z_LO + owner // near) * owned + node % owned
    owners_copy.wait()
    recv = dot(selector(where, owners.shape[0]), owners[...]).astype(jnp.bfloat16)
    pre += dot(recv[:, :width], w_in[2 * width :, :])
    pre += b_in
    sigma = jax.nn.sigmoid(pre)
    hidden = (pre * sigma).astype(jnp.bfloat16)
    outer = dot(hidden, w_out[...]) + b_out
    center = outer - jnp.mean(outer, axis=1, keepdims=True)
    inv_std = lax.rsqrt(jnp.mean(center * center, axis=1, keepdims=True) + 1e-05)
    normed = center * inv_std
    message = jnp.where(alive, normed * gain + bias, 0.0).astype(jnp.bfloat16)
    packed[:, :width] = message
    new_edges[...] = (edges[...].astype(jnp.float32) + message.astype(jnp.float32)).astype(jnp.bfloat16)
    cot_copy.wait()
    cot = edge_cot[...].astype(jnp.float32) + recv[:, width:].astype(jnp.float32)
    scaled = jnp.where(alive, cot, 0.0) * gain
    d_outer = inv_std * (
        scaled
        - jnp.mean(scaled, axis=1, keepdims=True)
        - normed * jnp.mean(scaled * normed, axis=1, keepdims=True)
    )
    d_hidden = dot_t(d_outer.astype(jnp.bfloat16), w_out[...])
    d_pre = (d_hidden * sigma * (1.0 + pre * (1.0 - sigma))).astype(jnp.bfloat16)
    packed[:, width : 2 * width] = d_pre
    packed[:, 2 * width :] = jnp.broadcast_to(
        (node % owned).astype(jnp.float32), (slots, packed.shape[1] - 2 * width)
    ).astype(jnp.bfloat16)
    row = lax.broadcasted_iota(jnp.int32, (group, slots), 0)
    placed = jnp.where(spread[...] == row, 1.0, 0.0).astype(jnp.bfloat16)
    partial[...] = dot(placed, d_pre).astype(jnp.bfloat16)


def owner_kernel(returned, column_sum, to_below, to_above, w_in, aggregated, grad_nodes):
    owned, width = aggregated.shape
    index = returned[:, 2 * width :].astype(jnp.float32)
    lane = lax.broadcasted_iota(jnp.int32, index.shape, 1).astype(jnp.float32)
    onehot = jnp.where(index == lane, 1.0, 0.0).astype(jnp.bfloat16)
    summed = lax.dot_general(
        onehot, returned[:, : 2 * width], (((0,), (0,)), ((), ())), preferred_element_type=jnp.float32
    )[:owned]
    aggregated[...] = summed[:, :width].astype(jnp.bfloat16)
    sent = column_sum[:owned, :] + to_below[...].astype(jnp.float32) + to_above[...].astype(jnp.float32)
    grad = dot_t(sent.astype(jnp.bfloat16), w_in[width : 2 * width, :])
    grad += dot_t(summed[:, width:].astype(jnp.bfloat16), w_in[2 * width :, :])
    grad_nodes[...] = grad.astype(jnp.bfloat16)


VMEM = pl.BlockSpec(memory_space=pltpu.VMEM)
HBM = pl.BlockSpec(memory_space=pltpu.HBM)


def everywhere(block, axis, groups):
    peers = len(groups[0])
    copies = jnp.broadcast_to(block[None], (peers,) + block.shape).reshape(-1, block.shape[1])
    return lax.all_to_all(copies, axis, 0, 0, tiled=True, axis_index_groups=groups)


def on_device(
    node_latents,
    edge_latents,
    edge_sender,
    edge_receiver,
    edge_count,
    w_in,
    b_in,
    w_out,
    b_out,
    ln_gain,
    ln_bias,
    agg_cotangent,
    edge_cotangent,
):
    owned, width = node_latents.shape
    slots = edge_latents.shape[0]
    rows = lax.axis_size("row")
    cols = lax.axis_size("col")
    tall, near = cols // Z_HI, rows // Z_LO
    along_y = [[y * Z_HI + h for y in range(tall)] for h in range(Z_HI)]
    along_h = [[y * Z_HI + h for h in range(Z_HI)] for y in range(tall)]
    along_z = [[z * near + n for z in range(Z_LO)] for n in range(near)]
    along_x = [[z * near + n for n in range(near)] for z in range(Z_LO)]
    up = [(y * Z_HI + h, y * Z_HI + (h + 1) % Z_HI) for y in range(tall) for h in range(Z_HI)]
    down = [(b, a) for a, b in up]
    my_h = lax.axis_index("col") % Z_HI

    own = jnp.concatenate([node_latents, agg_cotangent], axis=1)
    quarter = everywhere(own, "row", along_z)
    owners = lax.all_gather(quarter, "row", axis=0, tiled=True, axis_index_groups=along_x)
    mine, quarter = lax.optimization_barrier((node_latents, quarter))
    senders = everywhere(everywhere(mine, "col", along_h), "col", along_y)

    device = edge_sender // owned
    turn = (my_h - device % Z_HI + Z_HI) % Z_HI
    place = ((device // Z_HI) * Z_HI + turn) * owned + edge_sender % owned
    vectors = jnp.stack([b_in, b_out, ln_gain, ln_bias])

    new_edges, packed, partial = pl.pallas_call(
        edge_kernel,
        in_specs=[VMEM] * 8 + [HBM] * 3,
        out_specs=[VMEM] * 3,
        out_shape=[
            jax.ShapeDtypeStruct((slots, width), jnp.bfloat16),
            jax.ShapeDtypeStruct((slots, 2 * width + 128), jnp.bfloat16),
            jax.ShapeDtypeStruct((cols * owned, width), jnp.bfloat16),
        ],
        scratch_shapes=[
            pltpu.VMEM((rows * owned, 2 * width), jnp.bfloat16),
            pltpu.VMEM((slots, width), jnp.bfloat16),
            pltpu.VMEM((slots, width), jnp.bfloat16),
            pltpu.SemaphoreType.DMA((3,)),
        ],
        compiler_params=pltpu.CompilerParams(vmem_limit_bytes=40 * 1024 * 1024),
        cost_estimate=pl.CostEstimate(
            flops=2 * slots * width * (5 * width + 2 * cols * owned + 2 * rows * owned),
            bytes_accessed=8 * 1024 * 1024,
            transcendentals=slots * width,
        ),
    )(
        senders, edge_sender.reshape(1, slots), place.reshape(1, slots), edge_receiver.reshape(1, slots),
        edge_count, w_in, w_out, vectors, owners, edge_latents, edge_cotangent,
    )

    parts = lax.all_to_all(partial, "col", 0, 0, tiled=True, axis_index_groups=along_y)
    column_sum = jnp.sum(parts.reshape(tall, Z_HI * owned, width).astype(jnp.float32), axis=0)
    away = column_sum.astype(jnp.bfloat16)
    to_below = lax.ppermute(away[owned : 2 * owned], "col", down)
    to_above = lax.ppermute(away[2 * owned :], "col", up)

    returned = lax.all_to_all(packed, "row", 0, 0, tiled=True)
    aggregated, grad_nodes = pl.pallas_call(
        owner_kernel,
        in_specs=[VMEM] * 5,
        out_specs=[VMEM] * 2,
        out_shape=[jax.ShapeDtypeStruct((owned, width), jnp.bfloat16)] * 2,
        cost_estimate=pl.CostEstimate(
            flops=2 * owned * width * (2 * slots + 2 * width), bytes_accessed=2 * 1024 * 1024, transcendentals=0
        ),
    )(returned, column_sum, to_below, to_above, w_in)
    d_edge = dot_t(packed[:, width : 2 * width], w_in[:width])
    grad_edges = (edge_cotangent.astype(jnp.float32) + d_edge).astype(jnp.bfloat16)
    return (new_edges, aggregated, grad_nodes, grad_edges)


def solution(mesh):
    split = P(("row", "col"), None)
    return jax.shard_map(
        on_device,
        mesh=mesh,
        in_specs=(
            split, split, P(("row", "col")), P(("row", "col")), split,
            P(), P(), P(), P(), P(), P(), split, split,
        ),
        out_specs=(split, split, split, split),
        check_vma=False,
    )
```

```python
import functools

import jax
import jax.numpy as jnp
from jax import lax
from jax.experimental import pallas as pl
from jax.experimental.pallas import tpu as pltpu
from jax.sharding import PartitionSpec as P

Z_HI = 3


def dot(a, b):
    return jnp.dot(a, b, preferred_element_type=jnp.float32)


def dot_t(a, b):
    return lax.dot_general(a, b, (((1,), (1,)), ((), ())), preferred_element_type=jnp.float32)


def onehot_of(asked, owned):
    rows, _, per_block = asked.shape
    spread = jnp.broadcast_to(asked[...], (rows, per_block, per_block)).reshape(rows * per_block, per_block)
    slot = lax.broadcasted_iota(jnp.int32, spread.shape, 0) % per_block
    lane = lax.broadcasted_iota(jnp.int32, spread.shape, 1)
    index = jnp.sum(jnp.where(slot == lane, spread, 0), axis=1, keepdims=True)
    node = lax.broadcasted_iota(jnp.int32, (rows * per_block, owned), 1)
    return jnp.where(index % owned == node, 1.0, 0.0).astype(jnp.bfloat16)


def answer_kernel(asked, own, answer):
    answer[...] = dot(onehot_of(asked, own.shape[0]), own[...]).astype(jnp.bfloat16)


def edge_kernel(
    table, spread, recv, counts, w_in, w_out, vectors, edges_hbm, cot_hbm,
    new_edges, packed, partial,
    edges, edge_cot, sems,
):
    slots, width = edges.shape
    group = table.shape[0]
    per_block = slots // counts.shape[1]
    edges_copy = pltpu.make_async_copy(edges_hbm, edges, sems.at[0])
    cot_copy = pltpu.make_async_copy(cot_hbm, edge_cot, sems.at[1])
    edges_copy.start()
    cot_copy.start()
    b_in, b_out = vectors[0:1, :], vectors[1:2, :]
    gain, bias = vectors[2:3, :], vectors[3:4, :]
    diagonal = lax.broadcasted_iota(jnp.int32, (slots, slots), 0) == lax.broadcasted_iota(
        jnp.int32, (slots, slots), 1
    )
    pick = jnp.sum(jnp.where(diagonal, spread[...], 0), axis=1, keepdims=True)
    slot = lax.broadcasted_iota(jnp.int32, (slots, counts.shape[1]), 0)
    block = lax.broadcasted_iota(jnp.int32, (slots, counts.shape[1]), 1)
    count = jnp.sum(jnp.where(slot // per_block == block, counts[...], 0), axis=1, keepdims=True)
    alive = slot[:, :1] % per_block < count
    lane = lax.broadcasted_iota(jnp.int32, (slots, group), 1)
    chosen = jnp.where(pick == lane, 1.0, 0.0).astype(jnp.bfloat16)
    send_feat = dot(chosen, table[...]).astype(jnp.bfloat16)
    pre = dot(recv[:, :width], w_in[2 * width :, :])
    pre += dot(send_feat, w_in[width : 2 * width, :])
    edges_copy.wait()
    pre += dot(edges[...], w_in[:width, :])
    pre += b_in
    sigma = jax.nn.sigmoid(pre)
    hidden = (pre * sigma).astype(jnp.bfloat16)
    outer = dot(hidden, w_out[...]) + b_out
    center = outer - jnp.mean(outer, axis=1, keepdims=True)
    inv_std = lax.rsqrt(jnp.mean(center * center, axis=1, keepdims=True) + 1e-05)
    normed = center * inv_std
    message = jnp.where(alive, normed * gain + bias, 0.0).astype(jnp.bfloat16)
    packed[:, :width] = message
    new_edges[...] = (edges[...].astype(jnp.float32) + message.astype(jnp.float32)).astype(jnp.bfloat16)
    cot_copy.wait()
    cot = edge_cot[...].astype(jnp.float32) + recv[:, width:].astype(jnp.float32)
    scaled = jnp.where(alive, cot, 0.0) * gain
    d_outer = inv_std * (
        scaled
        - jnp.mean(scaled, axis=1, keepdims=True)
        - normed * jnp.mean(scaled * normed, axis=1, keepdims=True)
    )
    d_hidden = dot_t(d_outer.astype(jnp.bfloat16), w_out[...])
    d_pre = (d_hidden * sigma * (1.0 + pre * (1.0 - sigma))).astype(jnp.bfloat16)
    packed[:, width:] = d_pre
    row = lax.broadcasted_iota(jnp.int32, (group, slots), 0)
    placed = jnp.where(spread[...] == row, 1.0, 0.0).astype(jnp.bfloat16)
    partial[...] = dot(placed, d_pre).astype(jnp.bfloat16)


def owner_kernel(asked, returned, column_sum, to_below, to_above, w_in, aggregated, grad_nodes):
    owned, width = aggregated.shape
    onehot = onehot_of(asked, owned)
    summed = lax.dot_general(
        onehot, returned[...], (((0,), (0,)), ((), ())), preferred_element_type=jnp.float32
    )
    aggregated[...] = summed[:, :width].astype(jnp.bfloat16)
    sent = column_sum[:owned, :] + to_below[...].astype(jnp.float32) + to_above[...].astype(jnp.float32)
    grad = dot_t(sent.astype(jnp.bfloat16), w_in[width : 2 * width, :])
    grad += dot_t(summed[:, width:].astype(jnp.bfloat16), w_in[2 * width :, :])
    grad_nodes[...] = grad.astype(jnp.bfloat16)


VMEM = pl.BlockSpec(memory_space=pltpu.VMEM)
ANY = pl.BlockSpec(memory_space=pl.ANY)


def on_device(
    node_latents,
    edge_latents,
    edge_sender,
    edge_receiver,
    edge_count,
    w_in,
    b_in,
    w_out,
    b_out,
    ln_gain,
    ln_bias,
    agg_cotangent,
    edge_cotangent,
):
    owned, width = node_latents.shape
    slots = edge_latents.shape[0]
    rows = lax.axis_size("row")
    cols = lax.axis_size("col")
    per_block = slots // rows
    tall = cols // Z_HI
    along_y = [[y * Z_HI + h for y in range(tall)] for h in range(Z_HI)]
    up = [(y * Z_HI + h, y * Z_HI + (h + 1) % Z_HI) for y in range(tall) for h in range(Z_HI)]
    down = [(b, a) for a, b in up]
    my_h = lax.axis_index("col") % Z_HI

    own = jnp.concatenate([node_latents, agg_cotangent], axis=1)
    latents, own = lax.optimization_barrier((node_latents, own))
    from_below = lax.ppermute(latents, "col", up)
    from_above = lax.ppermute(latents, "col", down)
    asked = lax.all_to_all(edge_receiver.reshape(rows, 1, per_block), "row", 0, 0, tiled=True)
    answer = pl.pallas_call(
        answer_kernel,
        in_specs=[VMEM] * 2,
        out_specs=VMEM,
        out_shape=jax.ShapeDtypeStruct((slots, 2 * width), jnp.bfloat16),
        cost_estimate=pl.CostEstimate(
            flops=4_000_000_000, bytes_accessed=640 * 1024, transcendentals=0
        ),
        compiler_params=pltpu.CompilerParams(vmem_limit_bytes=16 * 1024 * 1024),
    )(asked, own)
    answer, from_below, from_above = lax.optimization_barrier((answer, from_below, from_above))
    recv = lax.all_to_all(answer, "row", 0, 0, tiled=True)
    column = jnp.concatenate([node_latents, from_below, from_above], axis=0)
    table = lax.all_gather(column, "col", axis=0, tiled=True, axis_index_groups=along_y)

    device = edge_sender // owned
    turn = (my_h - device % Z_HI + Z_HI) % Z_HI
    place = ((device // Z_HI) * Z_HI + turn) * owned + edge_sender % owned
    vectors = jnp.stack([b_in, b_out, ln_gain, ln_bias])

    new_edges, packed, partial = pl.pallas_call(
        edge_kernel,
        in_specs=[VMEM] * 7 + [ANY] * 2,
        out_specs=[VMEM] * 3,
        out_shape=[
            jax.ShapeDtypeStruct((slots, width), jnp.bfloat16),
            jax.ShapeDtypeStruct((slots, 2 * width), jnp.bfloat16),
            jax.ShapeDtypeStruct((cols * owned, width), jnp.bfloat16),
        ],
        scratch_shapes=[
            pltpu.VMEM((slots, width), jnp.bfloat16),
            pltpu.VMEM((slots, width), jnp.bfloat16),
            pltpu.SemaphoreType.DMA((2,)),
        ],
        compiler_params=pltpu.CompilerParams(vmem_limit_bytes=40 * 1024 * 1024),
        cost_estimate=pl.CostEstimate(
            flops=2 * slots * width * (5 * width + 2 * cols * owned),
            bytes_accessed=6 * 1024 * 1024,
            transcendentals=slots * width,
        ),
    )(
        table, place.reshape(1, slots), recv, edge_count, w_in, w_out, vectors,
        edge_latents, edge_cotangent,
    )

    parts = lax.all_to_all(partial, "col", 0, 0, tiled=True, axis_index_groups=along_y)
    column_sum = jnp.sum(parts.reshape(tall, Z_HI * owned, width).astype(jnp.float32), axis=0)
    away = column_sum.astype(jnp.bfloat16)
    to_below = lax.ppermute(away[owned : 2 * owned], "col", down)
    to_above = lax.ppermute(away[2 * owned :], "col", up)

    returned = lax.all_to_all(packed, "row", 0, 0, tiled=True)
    aggregated, grad_nodes = pl.pallas_call(
        owner_kernel,
        in_specs=[VMEM] * 6,
        out_specs=[VMEM] * 2,
        out_shape=[jax.ShapeDtypeStruct((owned, width), jnp.bfloat16)] * 2,
        cost_estimate=pl.CostEstimate(
            flops=2 * owned * width * (2 * slots + 2 * width), bytes_accessed=2 * 1024 * 1024, transcendentals=0
        ),
        compiler_params=pltpu.CompilerParams(vmem_limit_bytes=16 * 1024 * 1024),
    )(asked, returned, column_sum, to_below, to_above, w_in)
    d_edge = dot_t(packed[:, width:], w_in[:width])
    grad_edges = (edge_cotangent.astype(jnp.float32) + d_edge).astype(jnp.bfloat16)
    return (new_edges, aggregated, grad_nodes, grad_edges)


def solution(mesh):
    split = P(("row", "col"), None)
    return jax.shard_map(
        on_device,
        mesh=mesh,
        in_specs=(
            split, split, P(("row", "col")), P(("row", "col")), split,
            P(), P(), P(), P(), P(), P(), split, split,
        ),
        out_specs=(split, split, split, split),
        check_vma=False,
    )
```

```python
import functools

import jax
import jax.numpy as jnp
from jax import lax
from jax.experimental import pallas as pl
from jax.experimental.pallas import tpu as pltpu
from jax.sharding import PartitionSpec as P

Z_HI = 3


def dot(a, b):
    return jnp.dot(a, b, preferred_element_type=jnp.float32)


def dot_t(a, b):
    return lax.dot_general(a, b, (((1,), (1,)), ((), ())), preferred_element_type=jnp.float32)


def onehot_of(asked, owned):
    rows, _, per_block = asked.shape
    spread = jnp.broadcast_to(asked[...], (rows, per_block, per_block)).reshape(rows * per_block, per_block)
    slot = lax.broadcasted_iota(jnp.int32, spread.shape, 0) % per_block
    lane = lax.broadcasted_iota(jnp.int32, spread.shape, 1)
    index = jnp.sum(jnp.where(slot == lane, spread, 0), axis=1, keepdims=True)
    node = lax.broadcasted_iota(jnp.int32, (rows * per_block, owned), 1)
    return jnp.where(index % owned == node, 1.0, 0.0).astype(jnp.bfloat16)


def answer_kernel(asked, own, answer):
    answer[...] = dot(onehot_of(asked, own.shape[0]), own[...]).astype(jnp.bfloat16)


def edge_kernel(
    table, spread, recv, counts, w_out, vectors, w_hbm, edges_hbm, cot_hbm,
    new_edges, packed, partial,
    w_in, edges, edge_cot, sems,
):
    slots, width = edges.shape
    group = table.shape[0]
    per_block = slots // counts.shape[1]
    edges_copy = pltpu.make_async_copy(edges_hbm, edges, sems.at[0])
    cot_copy = pltpu.make_async_copy(cot_hbm, edge_cot, sems.at[1])
    w_copies = [
        pltpu.make_async_copy(
            w_hbm.at[pl.ds(part * width, width), :], w_in.at[pl.ds(part * width, width), :], sems.at[2 + part]
        )
        for part in range(3)
    ]
    for copy in (w_copies[1], w_copies[2], edges_copy, w_copies[0], cot_copy):
        copy.start()
    b_in, b_out = vectors[0:1, :], vectors[1:2, :]
    gain, bias = vectors[2:3, :], vectors[3:4, :]
    diagonal = lax.broadcasted_iota(jnp.int32, (slots, slots), 0) == lax.broadcasted_iota(
        jnp.int32, (slots, slots), 1
    )
    pick = jnp.sum(jnp.where(diagonal, spread[...], 0), axis=1, keepdims=True)
    slot = lax.broadcasted_iota(jnp.int32, (slots, counts.shape[1]), 0)
    block = lax.broadcasted_iota(jnp.int32, (slots, counts.shape[1]), 1)
    count = jnp.sum(jnp.where(slot // per_block == block, counts[...], 0), axis=1, keepdims=True)
    alive = slot[:, :1] % per_block < count
    lane = lax.broadcasted_iota(jnp.int32, (slots, group), 1)
    chosen = jnp.where(pick == lane, 1.0, 0.0).astype(jnp.bfloat16)
    send_feat = dot(chosen, table[...]).astype(jnp.bfloat16)
    w_copies[1].wait()
    pre = dot(send_feat, w_in[width : 2 * width, :])
    w_copies[2].wait()
    pre += dot(recv[:, :width], w_in[2 * width :, :])
    edges_copy.wait()
    w_copies[0].wait()
    pre += dot(edges[...], w_in[:width, :])
    pre += b_in
    sigma = jax.nn.sigmoid(pre)
    hidden = (pre * sigma).astype(jnp.bfloat16)
    outer = dot(hidden, w_out[...]) + b_out
    center = outer - jnp.mean(outer, axis=1, keepdims=True)
    inv_std = lax.rsqrt(jnp.mean(center * center, axis=1, keepdims=True) + 1e-05)
    normed = center * inv_std
    message = jnp.where(alive, normed * gain + bias, 0.0).astype(jnp.bfloat16)
    packed[:, :width] = message
    new_edges[...] = (edges[...].astype(jnp.float32) + message.astype(jnp.float32)).astype(jnp.bfloat16)
    cot_copy.wait()
    cot = edge_cot[...].astype(jnp.float32) + recv[:, width:].astype(jnp.float32)
    scaled = jnp.where(alive, cot, 0.0) * gain
    d_outer = inv_std * (
        scaled
        - jnp.mean(scaled, axis=1, keepdims=True)
        - normed * jnp.mean(scaled * normed, axis=1, keepdims=True)
    )
    d_hidden = dot_t(d_outer.astype(jnp.bfloat16), w_out[...])
    d_pre = (d_hidden * sigma * (1.0 + pre * (1.0 - sigma))).astype(jnp.bfloat16)
    packed[:, width:] = d_pre
    row = lax.broadcasted_iota(jnp.int32, (group, slots), 0)
    placed = jnp.where(spread[...] == row, 1.0, 0.0).astype(jnp.bfloat16)
    partial[...] = dot(placed, d_pre).astype(jnp.bfloat16)


def owner_kernel(asked, returned, column_sum, to_below, to_above, w_in, aggregated, grad_nodes):
    owned, width = aggregated.shape
    onehot = onehot_of(asked, owned)
    summed = lax.dot_general(
        onehot, returned[...], (((0,), (0,)), ((), ())), preferred_element_type=jnp.float32
    )
    aggregated[...] = summed[:, :width].astype(jnp.bfloat16)
    sent = column_sum[:owned, :] + to_below[...].astype(jnp.float32) + to_above[...].astype(jnp.float32)
    grad = dot_t(sent.astype(jnp.bfloat16), w_in[width : 2 * width, :])
    grad += dot_t(summed[:, width:].astype(jnp.bfloat16), w_in[2 * width :, :])
    grad_nodes[...] = grad.astype(jnp.bfloat16)


VMEM = pl.BlockSpec(memory_space=pltpu.VMEM)
ANY = pl.BlockSpec(memory_space=pl.ANY)


def on_device(
    node_latents,
    edge_latents,
    edge_sender,
    edge_receiver,
    edge_count,
    w_in,
    b_in,
    w_out,
    b_out,
    ln_gain,
    ln_bias,
    agg_cotangent,
    edge_cotangent,
):
    owned, width = node_latents.shape
    slots = edge_latents.shape[0]
    rows = lax.axis_size("row")
    cols = lax.axis_size("col")
    per_block = slots // rows
    tall = cols // Z_HI
    along_y = [[y * Z_HI + h for y in range(tall)] for h in range(Z_HI)]
    up = [(y * Z_HI + h, y * Z_HI + (h + 1) % Z_HI) for y in range(tall) for h in range(Z_HI)]
    down = [(b, a) for a, b in up]
    my_h = lax.axis_index("col") % Z_HI

    own = jnp.concatenate([node_latents, agg_cotangent], axis=1)
    from_below = lax.ppermute(node_latents, "col", up)
    from_above = lax.ppermute(node_latents, "col", down)
    asked = lax.all_to_all(edge_receiver.reshape(rows, 1, per_block), "row", 0, 0, tiled=True)
    answer = pl.pallas_call(
        answer_kernel,
        in_specs=[VMEM] * 2,
        out_specs=VMEM,
        out_shape=jax.ShapeDtypeStruct((slots, 2 * width), jnp.bfloat16),
        cost_estimate=pl.CostEstimate(
            flops=4_000_000_000, bytes_accessed=640 * 1024, transcendentals=0
        ),
        compiler_params=pltpu.CompilerParams(vmem_limit_bytes=16 * 1024 * 1024),
    )(asked, own)
    answer, from_below, from_above = lax.optimization_barrier((answer, from_below, from_above))
    recv = lax.all_to_all(answer, "row", 0, 0, tiled=True)
    column = jnp.concatenate([node_latents, from_below, from_above], axis=0)
    table = lax.all_gather(column, "col", axis=0, tiled=True, axis_index_groups=along_y)

    device = edge_sender // owned
    turn = (my_h - device % Z_HI + Z_HI) % Z_HI
    place = ((device // Z_HI) * Z_HI + turn) * owned + edge_sender % owned
    vectors = jnp.stack([b_in, b_out, ln_gain, ln_bias])

    new_edges, packed, partial = pl.pallas_call(
        edge_kernel,
        in_specs=[VMEM] * 6 + [ANY] * 3,
        out_specs=[VMEM] * 3,
        out_shape=[
            jax.ShapeDtypeStruct((slots, width), jnp.bfloat16),
            jax.ShapeDtypeStruct((slots, 2 * width), jnp.bfloat16),
            jax.ShapeDtypeStruct((cols * owned, width), jnp.bfloat16),
        ],
        scratch_shapes=[
            pltpu.VMEM((3 * width, width), jnp.bfloat16),
            pltpu.VMEM((slots, width), jnp.bfloat16),
            pltpu.VMEM((slots, width), jnp.bfloat16),
            pltpu.SemaphoreType.DMA((5,)),
        ],
        compiler_params=pltpu.CompilerParams(vmem_limit_bytes=50 * 1024 * 1024),
        cost_estimate=pl.CostEstimate(
            flops=2 * slots * width * (5 * width + 2 * cols * owned),
            bytes_accessed=6 * 1024 * 1024,
            transcendentals=slots * width,
        ),
    )(
        table, place.reshape(1, slots), recv, edge_count, w_out, vectors,
        w_in, edge_latents, edge_cotangent,
    )

    parts = lax.all_to_all(partial, "col", 0, 0, tiled=True, axis_index_groups=along_y)
    column_sum = jnp.sum(parts.reshape(tall, Z_HI * owned, width).astype(jnp.float32), axis=0)
    away = column_sum.astype(jnp.bfloat16)
    to_below = lax.ppermute(away[owned : 2 * owned], "col", down)
    to_above = lax.ppermute(away[2 * owned :], "col", up)

    returned = lax.all_to_all(packed, "row", 0, 0, tiled=True)
    aggregated, grad_nodes = pl.pallas_call(
        owner_kernel,
        in_specs=[VMEM] * 6,
        out_specs=[VMEM] * 2,
        out_shape=[jax.ShapeDtypeStruct((owned, width), jnp.bfloat16)] * 2,
        cost_estimate=pl.CostEstimate(
            flops=2 * owned * width * (2 * slots + 2 * width), bytes_accessed=2 * 1024 * 1024, transcendentals=0
        ),
        compiler_params=pltpu.CompilerParams(vmem_limit_bytes=16 * 1024 * 1024),
    )(asked, returned, column_sum, to_below, to_above, w_in)
    d_edge = dot_t(packed[:, width:], w_in[:width])
    grad_edges = (edge_cotangent.astype(jnp.float32) + d_edge).astype(jnp.bfloat16)
    return (new_edges, aggregated, grad_nodes, grad_edges)


def solution(mesh):
    split = P(("row", "col"), None)
    return jax.shard_map(
        on_device,
        mesh=mesh,
        in_specs=(
            split, split, P(("row", "col")), P(("row", "col")), split,
            P(), P(), P(), P(), P(), P(), split, split,
        ),
        out_specs=(split, split, split, split),
        check_vma=False,
    )
```

```python
import functools

import jax
import jax.numpy as jnp
from jax import lax
from jax.experimental import pallas as pl
from jax.experimental.pallas import tpu as pltpu
from jax.sharding import PartitionSpec as P

Z_HI = 3
ROOM = 48
NOTE = 16


def dot(a, b):
    return jnp.dot(a, b, preferred_element_type=jnp.float32)


def dot_t(a, b):
    return lax.dot_general(a, b, (((1,), (1,)), ((), ())), preferred_element_type=jnp.float32)


def onehot_of(asked, owned):
    rows, _, per_block = asked.shape
    spread = jnp.broadcast_to(asked[...], (rows, per_block, per_block)).reshape(rows * per_block, per_block)
    slot = lax.broadcasted_iota(jnp.int32, spread.shape, 0) % per_block
    lane = lax.broadcasted_iota(jnp.int32, spread.shape, 1)
    index = jnp.sum(jnp.where(slot == lane, spread, 0), axis=1, keepdims=True)
    node = lax.broadcasted_iota(jnp.int32, (rows * per_block, owned), 1)
    return jnp.where(index % owned == node, 1.0, 0.0).astype(jnp.bfloat16)


def answer_kernel(asked, own, answer):
    answer[...] = dot(onehot_of(asked, own.shape[0]), own[...]).astype(jnp.bfloat16)


def column_of(row):
    n = row.shape[1]
    diagonal = lax.broadcasted_iota(jnp.int32, (n, n), 0) == lax.broadcasted_iota(jnp.int32, (n, n), 1)
    return jnp.sum(jnp.where(diagonal, row, 0), axis=1, keepdims=True)


def plan_kernel(room, height, nodes, cots, place, counts, own, note, target):
    width = nodes.shape[1]
    slots = place.shape[1]
    per_block = slots // counts.shape[1]
    own[:, :width] = nodes[...]
    own[:, width:] = cots[...]
    expand = (
        lax.broadcasted_iota(jnp.int32, (counts.shape[1], slots), 0)
        == lax.broadcasted_iota(jnp.int32, (counts.shape[1], slots), 1) // per_block
    )
    block_counts = column_of(counts[...])
    count = jnp.sum(jnp.where(expand, block_counts, 0), axis=0, keepdims=True)
    alive = lax.broadcasted_iota(jnp.int32, (1, slots), 1) % per_block < count
    neighbour = jnp.where(alive, place[...] // height, -1)
    inside = place[...] % height
    earlier = lax.broadcasted_iota(jnp.int32, (slots, slots), 0) < lax.broadcasted_iota(
        jnp.int32, (slots, slots), 1
    )
    same = (column_of(neighbour) == neighbour) & earlier
    rank = jnp.sum(jnp.where(same, 1, 0), axis=0, keepdims=True)
    fits = rank < room
    target[...] = jnp.where(alive & fits, neighbour * room + rank, -1)
    over = jnp.max(jnp.where(alive & jnp.logical_not(fits), 1.0, 0.0))
    chosen = jnp.where(
        target[...] == lax.broadcasted_iota(jnp.int32, (width, slots), 0), 1.0, 0.0
    ).astype(jnp.bfloat16)
    moved = dot_t(
        jnp.broadcast_to(inside.astype(jnp.float32), (NOTE, slots)).astype(jnp.bfloat16), chosen
    )
    first = lax.broadcasted_iota(jnp.int32, (NOTE, width), 0) == 0
    note[...] = jnp.where(first, over, moved).astype(jnp.bfloat16)


def edge_kernel(
    table, sender, target, recv, counts, w_out, vectors, w_hbm, edges_hbm, cot_hbm,
    new_edges, packed, compact, overflow,
    w_in, edges, edge_cot, sems,
):
    slots, width = edges.shape
    group = table.shape[0]
    sender_height = group // (compact.shape[0] // ROOM)
    per_block = slots // counts.shape[1]
    edges_copy = pltpu.make_async_copy(edges_hbm, edges, sems.at[0])
    cot_copy = pltpu.make_async_copy(cot_hbm, edge_cot, sems.at[1])
    w_copies = [
        pltpu.make_async_copy(
            w_hbm.at[pl.ds(part * width, width), :], w_in.at[pl.ds(part * width, width), :], sems.at[2 + part]
        )
        for part in range(3)
    ]
    for copy in (w_copies[1], w_copies[2], edges_copy, w_copies[0], cot_copy):
        copy.start()
    b_in, b_out = vectors[0:1, :], vectors[1:2, :]
    gain, bias = vectors[2:3, :], vectors[3:4, :]
    pick = column_of(sender[...])
    slot = lax.broadcasted_iota(jnp.int32, (slots, counts.shape[1]), 0)
    block = lax.broadcasted_iota(jnp.int32, (slots, counts.shape[1]), 1)
    count = jnp.sum(jnp.where(slot // per_block == block, counts[...], 0), axis=1, keepdims=True)
    alive = slot[:, :1] % per_block < count
    lane = lax.broadcasted_iota(jnp.int32, (slots, group), 1)
    chosen = jnp.where(pick == lane, 1.0, 0.0).astype(jnp.bfloat16)
    send_feat = dot(chosen, table[...]).astype(jnp.bfloat16)
    w_copies[1].wait()
    pre = dot(send_feat, w_in[width : 2 * width, :])
    w_copies[2].wait()
    pre += dot(recv[:, :width], w_in[2 * width :, :])
    edges_copy.wait()
    w_copies[0].wait()
    pre += dot(edges[...], w_in[:width, :])
    pre += b_in
    sigma = jax.nn.sigmoid(pre)
    hidden = (pre * sigma).astype(jnp.bfloat16)
    outer = dot(hidden, w_out[...]) + b_out
    center = outer - jnp.mean(outer, axis=1, keepdims=True)
    inv_std = lax.rsqrt(jnp.mean(center * center, axis=1, keepdims=True) + 1e-05)
    normed = center * inv_std
    message = jnp.where(alive, normed * gain + bias, 0.0).astype(jnp.bfloat16)
    packed[:, :width] = message
    new_edges[...] = (edges[...].astype(jnp.float32) + message.astype(jnp.float32)).astype(jnp.bfloat16)
    cot_copy.wait()
    cot = edge_cot[...].astype(jnp.float32) + recv[:, width:].astype(jnp.float32)
    scaled = jnp.where(alive, cot, 0.0) * gain
    d_outer = inv_std * (
        scaled
        - jnp.mean(scaled, axis=1, keepdims=True)
        - normed * jnp.mean(scaled * normed, axis=1, keepdims=True)
    )
    d_hidden = dot_t(d_outer.astype(jnp.bfloat16), w_out[...])
    d_pre = (d_hidden * sigma * (1.0 + pre * (1.0 - sigma))).astype(jnp.bfloat16)
    packed[:, width:] = d_pre
    row = lax.broadcasted_iota(jnp.int32, (compact.shape[0], slots), 0)
    chosen = jnp.where(target[...] == row, 1.0, 0.0).astype(jnp.bfloat16)
    compact[...] = dot(chosen, d_pre).astype(jnp.bfloat16)
    flags = sum(note[:, :128].astype(jnp.float32) for note in notes_of(table, sender_height))
    first = lax.broadcasted_iota(jnp.int32, flags.shape, 0) == 0
    overflow[0, 0] = (jnp.max(jnp.where(first, flags, 0.0)) > 0.5).astype(jnp.int32)


def notes_of(table, height):
    return [table[at + height - NOTE : at + height, :] for at in range(0, table.shape[0], height)]


def dense_kernel(packed, place, partial):
    width = partial.shape[1]
    row = lax.broadcasted_iota(jnp.int32, (partial.shape[0], packed.shape[0]), 0)
    placed = jnp.where(place[...] == row, 1.0, 0.0).astype(jnp.bfloat16)
    partial[...] = dot(placed, packed[:, width:]).astype(jnp.bfloat16)


def place_kernel(arrived, table, mine, column_sum):
    height, width = column_sum.shape
    notes = notes_of(table, height + NOTE)
    room = arrived.shape[0] // len(notes)
    shape = (NOTE, width)
    second = lax.broadcasted_iota(jnp.int32, shape, 0) == 1
    source = lax.broadcasted_iota(jnp.int32, shape, 0)
    index = jnp.zeros(shape, jnp.float32)
    for at, note in enumerate(notes):
        line = jnp.sum(jnp.where(second, note.astype(jnp.float32), 0.0), axis=0, keepdims=True)
        index = jnp.where(source == at, line, index)
    lane = lax.broadcasted_iota(jnp.int32, (width, 128), 0) - mine[0, 0] * room
    own_part = jnp.where(lane == lax.broadcasted_iota(jnp.int32, (width, 128), 1), 1.0, 0.0)
    index = dot(index.astype(jnp.bfloat16), own_part.astype(jnp.bfloat16))
    row = lax.broadcasted_iota(jnp.int32, (height, room), 0).astype(jnp.float32)
    total = jnp.zeros(column_sum.shape, jnp.float32)
    for at in range(len(notes)):
        placed = jnp.where(index[at : at + 1, :room] == row, 1.0, 0.0).astype(jnp.bfloat16)
        total += dot(placed, arrived[at * room : (at + 1) * room, :])
    column_sum[...] = total


def owner_kernel(asked, returned, column_sum, to_below, to_above, w_in, aggregated, grad_nodes):
    owned, width = aggregated.shape
    onehot = onehot_of(asked, owned)
    summed = lax.dot_general(
        onehot, returned[...], (((0,), (0,)), ((), ())), preferred_element_type=jnp.float32
    )
    aggregated[...] = summed[:, :width].astype(jnp.bfloat16)
    sent = column_sum[:owned, :] + to_below[...].astype(jnp.float32) + to_above[...].astype(jnp.float32)
    grad = dot_t(sent.astype(jnp.bfloat16), w_in[width : 2 * width, :])
    grad += dot_t(summed[:, width:].astype(jnp.bfloat16), w_in[2 * width :, :])
    grad_nodes[...] = grad.astype(jnp.bfloat16)


VMEM = pl.BlockSpec(memory_space=pltpu.VMEM)
ANY = pl.BlockSpec(memory_space=pl.ANY)


def on_device(
    node_latents,
    edge_latents,
    edge_sender,
    edge_receiver,
    edge_count,
    w_in,
    b_in,
    w_out,
    b_out,
    ln_gain,
    ln_bias,
    agg_cotangent,
    edge_cotangent,
):
    owned, width = node_latents.shape
    slots = edge_latents.shape[0]
    rows = lax.axis_size("row")
    cols = lax.axis_size("col")
    per_block = slots // rows
    tall = cols // Z_HI
    along_y = [[y * Z_HI + h for y in range(tall)] for h in range(Z_HI)]
    up = [(y * Z_HI + h, y * Z_HI + (h + 1) % Z_HI) for y in range(tall) for h in range(Z_HI)]
    down = [(b, a) for a, b in up]
    my_h = lax.axis_index("col") % Z_HI

    height = Z_HI * owned
    device = edge_sender // owned
    turn = (my_h - device % Z_HI + Z_HI) % Z_HI
    place = (device // Z_HI) * height + turn * owned + edge_sender % owned
    sender = (place + (device // Z_HI) * NOTE).reshape(1, slots)
    place = place.reshape(1, slots)
    own, note, target = pl.pallas_call(
        functools.partial(plan_kernel, ROOM, height),
        in_specs=[VMEM] * 4,
        out_specs=[VMEM] * 3,
        out_shape=[
            jax.ShapeDtypeStruct((owned, 2 * width), jnp.bfloat16),
            jax.ShapeDtypeStruct((NOTE, width), jnp.bfloat16),
            jax.ShapeDtypeStruct((1, slots), jnp.int32),
        ],
        cost_estimate=pl.CostEstimate(
            flops=2 * NOTE * slots * width, bytes_accessed=256 * 1024, transcendentals=0
        ),
        compiler_params=pltpu.CompilerParams(vmem_limit_bytes=16 * 1024 * 1024),
    )(node_latents, agg_cotangent, place, edge_count)
    from_below = lax.ppermute(node_latents, "col", up)
    from_above = lax.ppermute(node_latents, "col", down)
    asked = lax.all_to_all(edge_receiver.reshape(rows, 1, per_block), "row", 0, 0, tiled=True)
    answer = pl.pallas_call(
        answer_kernel,
        in_specs=[VMEM] * 2,
        out_specs=VMEM,
        out_shape=jax.ShapeDtypeStruct((slots, 2 * width), jnp.bfloat16),
        cost_estimate=pl.CostEstimate(
            flops=4_000_000_000, bytes_accessed=640 * 1024, transcendentals=0
        ),
        compiler_params=pltpu.CompilerParams(vmem_limit_bytes=16 * 1024 * 1024),
    )(asked, own)
    answer, from_below, from_above = lax.optimization_barrier((answer, from_below, from_above))
    recv = lax.all_to_all(answer, "row", 0, 0, tiled=True)
    column = jnp.concatenate([node_latents, from_below, from_above, note], axis=0)
    table = lax.all_gather(column, "col", axis=0, tiled=True, axis_index_groups=along_y)

    vectors = jnp.stack([b_in, b_out, ln_gain, ln_bias])

    new_edges, packed, compact, overflow = pl.pallas_call(
        edge_kernel,
        in_specs=[VMEM] * 7 + [ANY] * 3,
        out_specs=[VMEM] * 3 + [pl.BlockSpec(memory_space=pltpu.SMEM)],
        out_shape=[
            jax.ShapeDtypeStruct((slots, width), jnp.bfloat16),
            jax.ShapeDtypeStruct((slots, 2 * width), jnp.bfloat16),
            jax.ShapeDtypeStruct((tall * ROOM, width), jnp.bfloat16),
            jax.ShapeDtypeStruct((1, 1), jnp.int32),
        ],
        scratch_shapes=[
            pltpu.VMEM((3 * width, width), jnp.bfloat16),
            pltpu.VMEM((slots, width), jnp.bfloat16),
            pltpu.VMEM((slots, width), jnp.bfloat16),
            pltpu.SemaphoreType.DMA((5,)),
        ],
        compiler_params=pltpu.CompilerParams(vmem_limit_bytes=50 * 1024 * 1024),
        cost_estimate=pl.CostEstimate(
            flops=2 * slots * width * (5 * width + 2 * cols * owned),
            bytes_accessed=6 * 1024 * 1024,
            transcendentals=slots * width,
        ),
    )(
        table, sender, target, recv, edge_count, w_out, vectors,
        w_in, edge_latents, edge_cotangent,
    )

    def short_way():
        arrived = lax.all_to_all(compact, "col", 0, 0, tiled=True, axis_index_groups=along_y)
        mine = (lax.axis_index("col") // Z_HI).astype(jnp.int32).reshape(1, 1)
        return pl.pallas_call(
            place_kernel,
            in_specs=[VMEM] * 2 + [pl.BlockSpec(memory_space=pltpu.SMEM)],
            out_specs=VMEM,
            out_shape=jax.ShapeDtypeStruct((height, width), jnp.float32),
            compiler_params=pltpu.CompilerParams(vmem_limit_bytes=16 * 1024 * 1024),
        )(arrived, table, mine)

    def long_way():
        partial = pl.pallas_call(
            dense_kernel,
            in_specs=[VMEM] * 2,
            out_specs=VMEM,
            out_shape=jax.ShapeDtypeStruct((tall * height, width), jnp.bfloat16),
            compiler_params=pltpu.CompilerParams(vmem_limit_bytes=16 * 1024 * 1024),
        )(packed, place)
        parts = lax.all_to_all(partial, "col", 0, 0, tiled=True, axis_index_groups=along_y)
        return jnp.sum(parts.reshape(tall, height, width).astype(jnp.float32), axis=0)

    column_sum = lax.cond(overflow[0, 0] > 0, long_way, short_way)
    away = column_sum.astype(jnp.bfloat16)
    to_below = lax.ppermute(away[owned : 2 * owned], "col", down)
    to_above = lax.ppermute(away[2 * owned :], "col", up)

    returned = lax.all_to_all(packed, "row", 0, 0, tiled=True)
    aggregated, grad_nodes = pl.pallas_call(
        owner_kernel,
        in_specs=[VMEM] * 6,
        out_specs=[VMEM] * 2,
        out_shape=[jax.ShapeDtypeStruct((owned, width), jnp.bfloat16)] * 2,
        cost_estimate=pl.CostEstimate(
            flops=2 * owned * width * (2 * slots + 2 * width), bytes_accessed=2 * 1024 * 1024, transcendentals=0
        ),
        compiler_params=pltpu.CompilerParams(vmem_limit_bytes=16 * 1024 * 1024),
    )(asked, returned, column_sum, to_below, to_above, w_in)
    d_edge = dot_t(packed[:, width:], w_in[:width])
    grad_edges = (edge_cotangent.astype(jnp.float32) + d_edge).astype(jnp.bfloat16)
    return (new_edges, aggregated, grad_nodes, grad_edges)


def solution(mesh):
    split = P(("row", "col"), None)
    return jax.shard_map(
        on_device,
        mesh=mesh,
        in_specs=(
            split, split, P(("row", "col")), P(("row", "col")), split,
            P(), P(), P(), P(), P(), P(), split, split,
        ),
        out_specs=(split, split, split, split),
        check_vma=False,
    )
```

```python
import functools

import jax
import jax.numpy as jnp
from jax import lax
from jax.experimental import pallas as pl
from jax.experimental.pallas import tpu as pltpu
from jax.sharding import PartitionSpec as P

Z_HI = 3
ROOM = 48


def dot(a, b):
    return jnp.dot(a, b, preferred_element_type=jnp.float32)


def dot_t(a, b):
    return lax.dot_general(a, b, (((1,), (1,)), ((), ())), preferred_element_type=jnp.float32)


def onehot_of(asked, my_row, owned):
    rows, _, slots = asked.shape
    per_block = slots // rows
    shape = (rows * per_block, slots)
    spread = jnp.broadcast_to(asked[...], (rows, per_block, slots)).reshape(shape)
    wanted = my_row[0, 0] * per_block + lax.broadcasted_iota(jnp.int32, shape, 0) % per_block
    lane = lax.broadcasted_iota(jnp.int32, shape, 1)
    index = jnp.sum(jnp.where(wanted == lane, spread, 0), axis=1, keepdims=True)
    node = lax.broadcasted_iota(jnp.int32, (rows * per_block, owned), 1)
    return jnp.where(index % owned == node, 1.0, 0.0).astype(jnp.bfloat16)


def answer_kernel(asked, my_row, own, answer):
    answer[...] = dot(onehot_of(asked, my_row, own.shape[0]), own[...]).astype(jnp.bfloat16)


def column_of(row):
    n = row.shape[1]
    diagonal = lax.broadcasted_iota(jnp.int32, (n, n), 0) == lax.broadcasted_iota(jnp.int32, (n, n), 1)
    return jnp.sum(jnp.where(diagonal, row, 0), axis=1, keepdims=True)


def plan_kernel(height, nodes, cots, place, counts, own, note, target, rest):
    width = nodes.shape[1]
    slots = place.shape[1]
    per_block = slots // counts.shape[1]
    own[:, :width] = nodes[...]
    own[:, width:] = cots[...]
    expand = (
        lax.broadcasted_iota(jnp.int32, (counts.shape[1], slots), 0)
        == lax.broadcasted_iota(jnp.int32, (counts.shape[1], slots), 1) // per_block
    )
    block_counts = column_of(counts[...])
    count = jnp.sum(jnp.where(expand, block_counts, 0), axis=0, keepdims=True)
    alive = lax.broadcasted_iota(jnp.int32, (1, slots), 1) % per_block < count
    neighbour = jnp.where(alive, place[...] // height, -1)
    inside = place[...] % height
    earlier = lax.broadcasted_iota(jnp.int32, (slots, slots), 0) < lax.broadcasted_iota(
        jnp.int32, (slots, slots), 1
    )
    same = (column_of(neighbour) == neighbour) & earlier
    rank = jnp.sum(jnp.where(same, 1, 0), axis=0, keepdims=True)
    fits = alive & (rank < ROOM - 1)
    left = alive & (rank >= ROOM - 1)
    target[...] = jnp.where(fits, neighbour * ROOM + rank, -1)
    rest[...] = jnp.where(left, place[...], -1)
    over = jnp.max(jnp.where(left, 1.0, 0.0))
    shape = note.shape
    row = lax.broadcasted_iota(jnp.int32, (shape[0], slots), 0)
    told = (row % ROOM == ROOM - 1) & (row // ROOM == neighbour) & fits
    values = jnp.where(told, inside, 0).astype(jnp.float32).astype(jnp.bfloat16)
    at = lax.broadcasted_iota(jnp.int32, (width, slots), 0) == rank
    lines = dot_t(values, jnp.where(at, 1.0, 0.0).astype(jnp.bfloat16))
    flag = (lax.broadcasted_iota(jnp.int32, shape, 0) % ROOM == ROOM - 1) & (
        lax.broadcasted_iota(jnp.int32, shape, 1) == width - 1
    )
    note[...] = jnp.where(flag, over, lines).astype(jnp.bfloat16)


def edge_kernel(
    table, sender, target, note, recv, counts, w_out, vectors, w_hbm, edges_hbm, cot_hbm,
    new_edges, packed, compact,
    w_in, edges, edge_cot, sems,
):
    slots, width = edges.shape
    group = table.shape[0]
    per_block = slots // counts.shape[1]
    edges_copy = pltpu.make_async_copy(edges_hbm, edges, sems.at[0])
    cot_copy = pltpu.make_async_copy(cot_hbm, edge_cot, sems.at[1])
    w_copies = [
        pltpu.make_async_copy(
            w_hbm.at[pl.ds(part * width, width), :], w_in.at[pl.ds(part * width, width), :], sems.at[2 + part]
        )
        for part in range(3)
    ]
    for copy in (w_copies[1], w_copies[2], edges_copy, w_copies[0], cot_copy):
        copy.start()
    b_in, b_out = vectors[0:1, :], vectors[1:2, :]
    gain, bias = vectors[2:3, :], vectors[3:4, :]
    pick = column_of(sender[...])
    slot = lax.broadcasted_iota(jnp.int32, (slots, counts.shape[1]), 0)
    block = lax.broadcasted_iota(jnp.int32, (slots, counts.shape[1]), 1)
    count = jnp.sum(jnp.where(slot // per_block == block, counts[...], 0), axis=1, keepdims=True)
    alive = slot[:, :1] % per_block < count
    lane = lax.broadcasted_iota(jnp.int32, (slots, group), 1)
    chosen = jnp.where(pick == lane, 1.0, 0.0).astype(jnp.bfloat16)
    send_feat = dot(chosen, table[...]).astype(jnp.bfloat16)
    w_copies[1].wait()
    pre = dot(send_feat, w_in[width : 2 * width, :])
    w_copies[2].wait()
    pre += dot(recv[:, :width], w_in[2 * width :, :])
    edges_copy.wait()
    w_copies[0].wait()
    pre += dot(edges[...], w_in[:width, :])
    pre += b_in
    sigma = jax.nn.sigmoid(pre)
    hidden = (pre * sigma).astype(jnp.bfloat16)
    outer = dot(hidden, w_out[...]) + b_out
    center = outer - jnp.mean(outer, axis=1, keepdims=True)
    inv_std = lax.rsqrt(jnp.mean(center * center, axis=1, keepdims=True) + 1e-05)
    normed = center * inv_std
    message = jnp.where(alive, normed * gain + bias, 0.0).astype(jnp.bfloat16)
    packed[:, :width] = message
    new_edges[...] = (edges[...].astype(jnp.float32) + message.astype(jnp.float32)).astype(jnp.bfloat16)
    cot_copy.wait()
    cot = edge_cot[...].astype(jnp.float32) + recv[:, width:].astype(jnp.float32)
    scaled = jnp.where(alive, cot, 0.0) * gain
    d_outer = inv_std * (
        scaled
        - jnp.mean(scaled, axis=1, keepdims=True)
        - normed * jnp.mean(scaled * normed, axis=1, keepdims=True)
    )
    d_hidden = dot_t(d_outer.astype(jnp.bfloat16), w_out[...])
    d_pre = (d_hidden * sigma * (1.0 + pre * (1.0 - sigma))).astype(jnp.bfloat16)
    packed[:, width:] = d_pre
    row = lax.broadcasted_iota(jnp.int32, (compact.shape[0], slots), 0)
    chosen = jnp.where(target[...] == row, 1.0, 0.0).astype(jnp.bfloat16)
    compact[...] = (dot(chosen, d_pre) + note[...].astype(jnp.float32)).astype(jnp.bfloat16)


def dense_kernel(packed, place, partial):
    width = partial.shape[1]
    row = lax.broadcasted_iota(jnp.int32, (partial.shape[0], packed.shape[0]), 0)
    placed = jnp.where(place[...] == row, 1.0, 0.0).astype(jnp.bfloat16)
    partial[...] = dot(placed, packed[:, width:]).astype(jnp.bfloat16)


def place_kernel(arrived, column_sum, overflow):
    height, width = column_sum.shape
    row = lax.broadcasted_iota(jnp.int32, (height, ROOM), 0).astype(jnp.float32)
    data = lax.broadcasted_iota(jnp.int32, (height, ROOM), 1) < ROOM - 1
    last = lax.broadcasted_iota(jnp.int32, (16, width), 0) == 15
    total = jnp.zeros(column_sum.shape, jnp.float32)
    over = jnp.zeros((1, 128), jnp.float32)
    for at in range(0, arrived.shape[0], ROOM):
        note = arrived[at + ROOM - 16 : at + ROOM, :].astype(jnp.float32)
        line = jnp.sum(jnp.where(last, note, 0.0), axis=0, keepdims=True)
        placed = jnp.where((line[:, :ROOM] == row) & data, 1.0, 0.0).astype(jnp.bfloat16)
        total += dot(placed, arrived[at : at + ROOM, :])
        over = jnp.maximum(over, line[:, width - 128 :])
    column_sum[...] = total
    end = lax.broadcasted_iota(jnp.int32, over.shape, 1) == 127
    overflow[0, 0] = (jnp.max(jnp.where(end, over, 0.0)) > 0.5).astype(jnp.int32)


def owner_kernel(asked, my_row, returned, column_sum, to_below, to_above, w_in, aggregated, grad_nodes):
    owned, width = aggregated.shape
    onehot = onehot_of(asked, my_row, owned)
    summed = lax.dot_general(
        onehot, returned[...], (((0,), (0,)), ((), ())), preferred_element_type=jnp.float32
    )
    aggregated[...] = summed[:, :width].astype(jnp.bfloat16)
    sent = column_sum[:owned, :] + to_below[...].astype(jnp.float32) + to_above[...].astype(jnp.float32)
    grad = dot_t(sent.astype(jnp.bfloat16), w_in[width : 2 * width, :])
    grad += dot_t(summed[:, width:].astype(jnp.bfloat16), w_in[2 * width :, :])
    grad_nodes[...] = grad.astype(jnp.bfloat16)


VMEM = pl.BlockSpec(memory_space=pltpu.VMEM)
ANY = pl.BlockSpec(memory_space=pl.ANY)
SMEM = pl.BlockSpec(memory_space=pltpu.SMEM)


def on_device(
    node_latents,
    edge_latents,
    edge_sender,
    edge_receiver,
    edge_count,
    w_in,
    b_in,
    w_out,
    b_out,
    ln_gain,
    ln_bias,
    agg_cotangent,
    edge_cotangent,
):
    owned, width = node_latents.shape
    slots = edge_latents.shape[0]
    rows = lax.axis_size("row")
    cols = lax.axis_size("col")
    per_block = slots // rows
    tall = cols // Z_HI
    along_y = [[y * Z_HI + h for y in range(tall)] for h in range(Z_HI)]
    up = [(y * Z_HI + h, y * Z_HI + (h + 1) % Z_HI) for y in range(tall) for h in range(Z_HI)]
    down = [(b, a) for a, b in up]
    my_h = lax.axis_index("col") % Z_HI

    height = Z_HI * owned
    device = edge_sender // owned
    turn = (my_h - device % Z_HI + Z_HI) % Z_HI
    place = (device // Z_HI) * height + turn * owned + edge_sender % owned
    place = place.reshape(1, slots)
    own, note, target, rest = pl.pallas_call(
        functools.partial(plan_kernel, height),
        in_specs=[VMEM] * 4,
        out_specs=[VMEM] * 4,
        out_shape=[
            jax.ShapeDtypeStruct((owned, 2 * width), jnp.bfloat16),
            jax.ShapeDtypeStruct((tall * ROOM, width), jnp.bfloat16),
            jax.ShapeDtypeStruct((1, slots), jnp.int32),
            jax.ShapeDtypeStruct((1, slots), jnp.int32),
        ],
        cost_estimate=pl.CostEstimate(
            flops=2 * tall * ROOM * slots * width, bytes_accessed=256 * 1024, transcendentals=0
        ),
        compiler_params=pltpu.CompilerParams(vmem_limit_bytes=16 * 1024 * 1024),
    )(node_latents, agg_cotangent, place, edge_count)
    from_below = lax.ppermute(node_latents, "col", up)
    from_above = lax.ppermute(node_latents, "col", down)
    my_row = lax.axis_index("row").astype(jnp.int32).reshape(1, 1)
    indices = jnp.broadcast_to(edge_receiver.reshape(1, 1, slots), (rows, 1, slots))
    asked = lax.all_to_all(indices, "row", 0, 0, tiled=True)
    answer = pl.pallas_call(
        answer_kernel,
        in_specs=[VMEM, SMEM, VMEM],
        out_specs=VMEM,
        out_shape=jax.ShapeDtypeStruct((slots, 2 * width), jnp.bfloat16),
        cost_estimate=pl.CostEstimate(
            flops=4_000_000_000, bytes_accessed=640 * 1024, transcendentals=0
        ),
        compiler_params=pltpu.CompilerParams(vmem_limit_bytes=16 * 1024 * 1024),
    )(asked, my_row, own)
    answer, from_below, from_above = lax.optimization_barrier((answer, from_below, from_above))
    recv = lax.all_to_all(answer, "row", 0, 0, tiled=True)
    column = jnp.concatenate([node_latents, from_below, from_above], axis=0)
    table = lax.all_gather(column, "col", axis=0, tiled=True, axis_index_groups=along_y)

    vectors = jnp.stack([b_in, b_out, ln_gain, ln_bias])

    new_edges, packed, compact = pl.pallas_call(
        edge_kernel,
        in_specs=[VMEM] * 8 + [ANY] * 3,
        out_specs=[VMEM] * 3,
        out_shape=[
            jax.ShapeDtypeStruct((slots, width), jnp.bfloat16),
            jax.ShapeDtypeStruct((slots, 2 * width), jnp.bfloat16),
            jax.ShapeDtypeStruct((tall * ROOM, width), jnp.bfloat16),
        ],
        scratch_shapes=[
            pltpu.VMEM((3 * width, width), jnp.bfloat16),
            pltpu.VMEM((slots, width), jnp.bfloat16),
            pltpu.VMEM((slots, width), jnp.bfloat16),
            pltpu.SemaphoreType.DMA((5,)),
        ],
        compiler_params=pltpu.CompilerParams(vmem_limit_bytes=50 * 1024 * 1024),
        cost_estimate=pl.CostEstimate(
            flops=2 * slots * width * (5 * width + 2 * cols * owned),
            bytes_accessed=6 * 1024 * 1024,
            transcendentals=slots * width,
        ),
    )(
        table, place, target, note, recv, edge_count, w_out, vectors,
        w_in, edge_latents, edge_cotangent,
    )

    arrived = lax.all_to_all(compact, "col", 0, 0, tiled=True, axis_index_groups=along_y)
    column_sum, overflow = pl.pallas_call(
        place_kernel,
        in_specs=[VMEM],
        out_specs=[VMEM, SMEM],
        out_shape=[
            jax.ShapeDtypeStruct((height, width), jnp.float32),
            jax.ShapeDtypeStruct((1, 1), jnp.int32),
        ],
        compiler_params=pltpu.CompilerParams(vmem_limit_bytes=16 * 1024 * 1024),
    )(arrived)

    def with_rest():
        partial = pl.pallas_call(
            dense_kernel,
            in_specs=[VMEM] * 2,
            out_specs=VMEM,
            out_shape=jax.ShapeDtypeStruct((tall * height, width), jnp.bfloat16),
            compiler_params=pltpu.CompilerParams(vmem_limit_bytes=16 * 1024 * 1024),
        )(packed, rest)
        parts = lax.all_to_all(partial, "col", 0, 0, tiled=True, axis_index_groups=along_y)
        return column_sum + jnp.sum(parts.reshape(tall, height, width).astype(jnp.float32), axis=0)

    column_sum = lax.cond(overflow[0, 0] > 0, with_rest, lambda: column_sum)
    away = column_sum.astype(jnp.bfloat16)
    to_below = lax.ppermute(away[owned : 2 * owned], "col", down)
    to_above = lax.ppermute(away[2 * owned :], "col", up)

    returned = lax.all_to_all(packed, "row", 0, 0, tiled=True)
    aggregated, grad_nodes = pl.pallas_call(
        owner_kernel,
        in_specs=[VMEM, SMEM] + [VMEM] * 5,
        out_specs=[VMEM] * 2,
        out_shape=[jax.ShapeDtypeStruct((owned, width), jnp.bfloat16)] * 2,
        cost_estimate=pl.CostEstimate(
            flops=2 * owned * width * (2 * slots + 2 * width), bytes_accessed=2 * 1024 * 1024, transcendentals=0
        ),
        compiler_params=pltpu.CompilerParams(vmem_limit_bytes=16 * 1024 * 1024),
    )(asked, my_row, returned, column_sum, to_below, to_above, w_in)
    d_edge = dot_t(packed[:, width:], w_in[:width])
    grad_edges = (edge_cotangent.astype(jnp.float32) + d_edge).astype(jnp.bfloat16)
    return (new_edges, aggregated, grad_nodes, grad_edges)


def solution(mesh):
    split = P(("row", "col"), None)
    return jax.shard_map(
        on_device,
        mesh=mesh,
        in_specs=(
            split, split, P(("row", "col")), P(("row", "col")), split,
            P(), P(), P(), P(), P(), P(), split, split,
        ),
        out_specs=(split, split, split, split),
        check_vma=False,
    )
```

```python
import functools

import jax
import jax.numpy as jnp
from jax import lax
from jax.experimental import pallas as pl
from jax.experimental.pallas import tpu as pltpu
from jax.sharding import PartitionSpec as P

Z_HI = 3
ROOM = 48


def dot(a, b):
    return jnp.dot(a, b, preferred_element_type=jnp.float32)


def dot_t(a, b):
    return lax.dot_general(a, b, (((1,), (1,)), ((), ())), preferred_element_type=jnp.float32)


def onehot_of(asked, my_row, owned):
    rows, _, slots = asked.shape
    per_block = slots // rows
    shape = (rows * per_block, slots)
    spread = jnp.broadcast_to(asked[...], (rows, per_block, slots)).reshape(shape)
    wanted = my_row[0, 0] * per_block + lax.broadcasted_iota(jnp.int32, shape, 0) % per_block
    lane = lax.broadcasted_iota(jnp.int32, shape, 1)
    index = jnp.sum(jnp.where(wanted == lane, spread, 0), axis=1, keepdims=True)
    node = lax.broadcasted_iota(jnp.int32, (rows * per_block, owned), 1)
    return jnp.where(index % owned == node, 1.0, 0.0).astype(jnp.bfloat16)


def answer_kernel(asked, my_row, own, answer):
    answer[...] = dot(onehot_of(asked, my_row, own.shape[0]), own[...]).astype(jnp.bfloat16)


def column_of(row):
    n = row.shape[1]
    diagonal = lax.broadcasted_iota(jnp.int32, (n, n), 0) == lax.broadcasted_iota(jnp.int32, (n, n), 1)
    return jnp.sum(jnp.where(diagonal, row, 0), axis=1, keepdims=True)


def plan_kernel(height, nodes, cots, place, counts, own, note, target, rest):
    width = nodes.shape[1]
    slots = place.shape[1]
    per_block = slots // counts.shape[1]
    own[:, :width] = nodes[...]
    own[:, width:] = cots[...]
    expand = (
        lax.broadcasted_iota(jnp.int32, (counts.shape[1], slots), 0)
        == lax.broadcasted_iota(jnp.int32, (counts.shape[1], slots), 1) // per_block
    )
    block_counts = column_of(counts[...])
    count = jnp.sum(jnp.where(expand, block_counts, 0), axis=0, keepdims=True)
    alive = lax.broadcasted_iota(jnp.int32, (1, slots), 1) % per_block < count
    neighbour = jnp.where(alive, place[...] // height, -1)
    inside = place[...] % height
    earlier = lax.broadcasted_iota(jnp.int32, (slots, slots), 0) < lax.broadcasted_iota(
        jnp.int32, (slots, slots), 1
    )
    same = (column_of(neighbour) == neighbour) & earlier
    rank = jnp.sum(jnp.where(same, 1, 0), axis=0, keepdims=True)
    fits = alive & (rank < ROOM - 1)
    left = alive & (rank >= ROOM - 1)
    target[...] = jnp.where(fits, neighbour * ROOM + rank, -1)
    rest[...] = jnp.where(left, place[...], -1)
    over = jnp.max(jnp.where(left, 1.0, 0.0))
    shape = note.shape
    row = lax.broadcasted_iota(jnp.int32, (shape[0], slots), 0)
    told = (row % ROOM == ROOM - 1) & (row // ROOM == neighbour) & fits
    values = jnp.where(told, inside, 0).astype(jnp.float32).astype(jnp.bfloat16)
    at = lax.broadcasted_iota(jnp.int32, (width, slots), 0) == rank
    lines = dot_t(values, jnp.where(at, 1.0, 0.0).astype(jnp.bfloat16))
    flag = (lax.broadcasted_iota(jnp.int32, shape, 0) % ROOM == ROOM - 1) & (
        lax.broadcasted_iota(jnp.int32, shape, 1) == width - 1
    )
    note[...] = jnp.where(flag, over, lines).astype(jnp.bfloat16)


def edge_kernel(
    table, sender, target, note, recv, counts, w_out, vectors, w_hbm, edges_hbm, cot_hbm,
    new_edges, packed, compact,
    w_in, edges, edge_cot, sems,
):
    slots, width = edges.shape
    group = table.shape[0]
    per_block = slots // counts.shape[1]
    edges_copy = pltpu.make_async_copy(edges_hbm, edges, sems.at[0])
    cot_copy = pltpu.make_async_copy(cot_hbm, edge_cot, sems.at[1])
    w_copies = [
        pltpu.make_async_copy(
            w_hbm.at[pl.ds(part * width, width), :], w_in.at[pl.ds(part * width, width), :], sems.at[2 + part]
        )
        for part in range(3)
    ]
    for copy in (w_copies[1], w_copies[2], edges_copy, w_copies[0], cot_copy):
        copy.start()
    b_in, b_out = vectors[0:1, :], vectors[1:2, :]
    gain, bias = vectors[2:3, :], vectors[3:4, :]
    pick = column_of(sender[...])
    slot = lax.broadcasted_iota(jnp.int32, (slots, counts.shape[1]), 0)
    block = lax.broadcasted_iota(jnp.int32, (slots, counts.shape[1]), 1)
    count = jnp.sum(jnp.where(slot // per_block == block, counts[...], 0), axis=1, keepdims=True)
    alive = slot[:, :1] % per_block < count
    lane = lax.broadcasted_iota(jnp.int32, (slots, group), 1)
    chosen = jnp.where(pick == lane, 1.0, 0.0).astype(jnp.bfloat16)
    send_feat = dot(chosen, table[...]).astype(jnp.bfloat16)
    w_copies[1].wait()
    pre = dot(send_feat, w_in[width : 2 * width, :])
    w_copies[2].wait()
    pre += dot(recv[:, :width], w_in[2 * width :, :])
    edges_copy.wait()
    w_copies[0].wait()
    pre += dot(edges[...], w_in[:width, :])
    pre += b_in
    sigma = jax.nn.sigmoid(pre)
    hidden = (pre * sigma).astype(jnp.bfloat16)
    outer = dot(hidden, w_out[...]) + b_out
    center = outer - jnp.mean(outer, axis=1, keepdims=True)
    inv_std = lax.rsqrt(jnp.mean(center * center, axis=1, keepdims=True) + 1e-05)
    normed = center * inv_std
    message = jnp.where(alive, normed * gain + bias, 0.0).astype(jnp.bfloat16)
    packed[:, :width] = message
    new_edges[...] = (edges[...].astype(jnp.float32) + message.astype(jnp.float32)).astype(jnp.bfloat16)
    cot_copy.wait()
    cot = edge_cot[...].astype(jnp.float32) + recv[:, width:].astype(jnp.float32)
    scaled = jnp.where(alive, cot, 0.0) * gain
    d_outer = inv_std * (
        scaled
        - jnp.mean(scaled, axis=1, keepdims=True)
        - normed * jnp.mean(scaled * normed, axis=1, keepdims=True)
    )
    d_hidden = dot_t(d_outer.astype(jnp.bfloat16), w_out[...])
    d_pre = (d_hidden * sigma * (1.0 + pre * (1.0 - sigma))).astype(jnp.bfloat16)
    packed[:, width:] = d_pre
    row = lax.broadcasted_iota(jnp.int32, (compact.shape[0], slots), 0)
    chosen = jnp.where(target[...] == row, 1.0, 0.0).astype(jnp.bfloat16)
    compact[...] = (dot(chosen, d_pre) + note[...].astype(jnp.float32)).astype(jnp.bfloat16)


def dense_kernel(packed, place, partial):
    width = partial.shape[1]
    row = lax.broadcasted_iota(jnp.int32, (partial.shape[0], packed.shape[0]), 0)
    placed = jnp.where(place[...] == row, 1.0, 0.0).astype(jnp.bfloat16)
    partial[...] = dot(placed, packed[:, width:]).astype(jnp.bfloat16)


def place_kernel(arrived, column_sum, overflow):
    height, width = column_sum.shape
    row = lax.broadcasted_iota(jnp.int32, (height, ROOM), 0).astype(jnp.float32)
    data = lax.broadcasted_iota(jnp.int32, (height, ROOM), 1) < ROOM - 1
    last = lax.broadcasted_iota(jnp.int32, (16, width), 0) == 15
    total = jnp.zeros(column_sum.shape, jnp.float32)
    over = jnp.zeros((1, 128), jnp.float32)
    for at in range(0, arrived.shape[0], ROOM):
        note = arrived[at + ROOM - 16 : at + ROOM, :].astype(jnp.float32)
        line = jnp.sum(jnp.where(last, note, 0.0), axis=0, keepdims=True)
        placed = jnp.where((line[:, :ROOM] == row) & data, 1.0, 0.0).astype(jnp.bfloat16)
        total += dot(placed, arrived[at : at + ROOM, :])
        over = jnp.maximum(over, line[:, width - 128 :])
    column_sum[...] = total
    end = lax.broadcasted_iota(jnp.int32, over.shape, 1) == 127
    overflow[0, 0] = (jnp.max(jnp.where(end, over, 0.0)) > 0.5).astype(jnp.int32)


def owner_kernel(asked, my_row, returned, column_sum, to_below, to_above, w_in, aggregated, grad_nodes):
    owned, width = aggregated.shape
    onehot = onehot_of(asked, my_row, owned)
    summed = lax.dot_general(
        onehot, returned[...], (((0,), (0,)), ((), ())), preferred_element_type=jnp.float32
    )
    aggregated[...] = summed[:, :width].astype(jnp.bfloat16)
    sent = column_sum[:owned, :] + to_below[...].astype(jnp.float32) + to_above[...].astype(jnp.float32)
    grad = dot_t(sent.astype(jnp.bfloat16), w_in[width : 2 * width, :])
    grad += dot_t(summed[:, width:].astype(jnp.bfloat16), w_in[2 * width :, :])
    grad_nodes[...] = grad.astype(jnp.bfloat16)


VMEM = pl.BlockSpec(memory_space=pltpu.VMEM)
ANY = pl.BlockSpec(memory_space=pl.ANY)
SMEM = pl.BlockSpec(memory_space=pltpu.SMEM)


def on_device(
    node_latents,
    edge_latents,
    edge_sender,
    edge_receiver,
    edge_count,
    w_in,
    b_in,
    w_out,
    b_out,
    ln_gain,
    ln_bias,
    agg_cotangent,
    edge_cotangent,
):
    owned, width = node_latents.shape
    slots = edge_latents.shape[0]
    rows = lax.axis_size("row")
    cols = lax.axis_size("col")
    per_block = slots // rows
    tall = cols // Z_HI
    along_y = [[y * Z_HI + h for y in range(tall)] for h in range(Z_HI)]
    up = [(y * Z_HI + h, y * Z_HI + (h + 1) % Z_HI) for y in range(tall) for h in range(Z_HI)]
    down = [(b, a) for a, b in up]
    my_h = lax.axis_index("col") % Z_HI

    height = Z_HI * owned
    device = edge_sender // owned
    turn = (my_h - device % Z_HI + Z_HI) % Z_HI
    place = (device // Z_HI) * height + turn * owned + edge_sender % owned
    place = place.reshape(1, slots)
    own, note, target, rest = pl.pallas_call(
        functools.partial(plan_kernel, height),
        in_specs=[VMEM] * 4,
        out_specs=[VMEM] * 4,
        out_shape=[
            jax.ShapeDtypeStruct((owned, 2 * width), jnp.bfloat16),
            jax.ShapeDtypeStruct((tall * ROOM, width), jnp.bfloat16),
            jax.ShapeDtypeStruct((1, slots), jnp.int32),
            jax.ShapeDtypeStruct((1, slots), jnp.int32),
        ],
        cost_estimate=pl.CostEstimate(
            flops=2 * tall * ROOM * slots * width, bytes_accessed=256 * 1024, transcendentals=0
        ),
        compiler_params=pltpu.CompilerParams(vmem_limit_bytes=16 * 1024 * 1024),
    )(node_latents, agg_cotangent, place, edge_count)
    from_below = lax.ppermute(node_latents, "col", up)
    indices = jnp.broadcast_to(edge_receiver.reshape(1, 1, slots), (rows, 1, slots))
    latents, indices = lax.optimization_barrier((node_latents, indices))
    from_above = lax.ppermute(latents, "col", down)
    my_row = lax.axis_index("row").astype(jnp.int32).reshape(1, 1)
    asked = lax.all_to_all(indices, "row", 0, 0, tiled=True)
    answer = pl.pallas_call(
        answer_kernel,
        in_specs=[VMEM, SMEM, VMEM],
        out_specs=VMEM,
        out_shape=jax.ShapeDtypeStruct((slots, 2 * width), jnp.bfloat16),
        cost_estimate=pl.CostEstimate(
            flops=4_000_000_000, bytes_accessed=640 * 1024, transcendentals=0
        ),
        compiler_params=pltpu.CompilerParams(vmem_limit_bytes=16 * 1024 * 1024),
    )(asked, my_row, own)
    answer, from_below, from_above = lax.optimization_barrier((answer, from_below, from_above))
    recv = lax.all_to_all(answer, "row", 0, 0, tiled=True)
    column = jnp.concatenate([node_latents, from_below, from_above], axis=0)
    table = lax.all_gather(column, "col", axis=0, tiled=True, axis_index_groups=along_y)

    vectors = jnp.stack([b_in, b_out, ln_gain, ln_bias])

    new_edges, packed, compact = pl.pallas_call(
        edge_kernel,
        in_specs=[VMEM] * 8 + [ANY] * 3,
        out_specs=[VMEM] * 3,
        out_shape=[
            jax.ShapeDtypeStruct((slots, width), jnp.bfloat16),
            jax.ShapeDtypeStruct((slots, 2 * width), jnp.bfloat16),
            jax.ShapeDtypeStruct((tall * ROOM, width), jnp.bfloat16),
        ],
        scratch_shapes=[
            pltpu.VMEM((3 * width, width), jnp.bfloat16),
            pltpu.VMEM((slots, width), jnp.bfloat16),
            pltpu.VMEM((slots, width), jnp.bfloat16),
            pltpu.SemaphoreType.DMA((5,)),
        ],
        compiler_params=pltpu.CompilerParams(vmem_limit_bytes=50 * 1024 * 1024),
        cost_estimate=pl.CostEstimate(
            flops=2 * slots * width * (5 * width + 2 * cols * owned),
            bytes_accessed=6 * 1024 * 1024,
            transcendentals=slots * width,
        ),
    )(
        table, place, target, note, recv, edge_count, w_out, vectors,
        w_in, edge_latents, edge_cotangent,
    )

    arrived = lax.all_to_all(compact, "col", 0, 0, tiled=True, axis_index_groups=along_y)
    column_sum, overflow = pl.pallas_call(
        place_kernel,
        in_specs=[VMEM],
        out_specs=[VMEM, SMEM],
        out_shape=[
            jax.ShapeDtypeStruct((height, width), jnp.float32),
            jax.ShapeDtypeStruct((1, 1), jnp.int32),
        ],
        compiler_params=pltpu.CompilerParams(vmem_limit_bytes=16 * 1024 * 1024),
    )(arrived)

    def with_rest():
        partial = pl.pallas_call(
            dense_kernel,
            in_specs=[VMEM] * 2,
            out_specs=VMEM,
            out_shape=jax.ShapeDtypeStruct((tall * height, width), jnp.bfloat16),
            compiler_params=pltpu.CompilerParams(vmem_limit_bytes=16 * 1024 * 1024),
        )(packed, rest)
        parts = lax.all_to_all(partial, "col", 0, 0, tiled=True, axis_index_groups=along_y)
        return column_sum + jnp.sum(parts.reshape(tall, height, width).astype(jnp.float32), axis=0)

    column_sum = lax.cond(overflow[0, 0] > 0, with_rest, lambda: column_sum)
    away = column_sum.astype(jnp.bfloat16)
    to_below = lax.ppermute(away[owned : 2 * owned], "col", down)
    to_above = lax.ppermute(away[2 * owned :], "col", up)

    returned = lax.all_to_all(packed, "row", 0, 0, tiled=True)
    aggregated, grad_nodes = pl.pallas_call(
        owner_kernel,
        in_specs=[VMEM, SMEM] + [VMEM] * 5,
        out_specs=[VMEM] * 2,
        out_shape=[jax.ShapeDtypeStruct((owned, width), jnp.bfloat16)] * 2,
        cost_estimate=pl.CostEstimate(
            flops=2 * owned * width * (2 * slots + 2 * width), bytes_accessed=2 * 1024 * 1024, transcendentals=0
        ),
        compiler_params=pltpu.CompilerParams(vmem_limit_bytes=16 * 1024 * 1024),
    )(asked, my_row, returned, column_sum, to_below, to_above, w_in)
    d_edge = dot_t(packed[:, width:], w_in[:width])
    grad_edges = (edge_cotangent.astype(jnp.float32) + d_edge).astype(jnp.bfloat16)
    return (new_edges, aggregated, grad_nodes, grad_edges)


def solution(mesh):
    split = P(("row", "col"), None)
    return jax.shard_map(
        on_device,
        mesh=mesh,
        in_specs=(
            split, split, P(("row", "col")), P(("row", "col")), split,
            P(), P(), P(), P(), P(), P(), split, split,
        ),
        out_specs=(split, split, split, split),
        check_vma=False,
    )
```

```python
import functools

import jax
import jax.numpy as jnp
from jax import lax
from jax.experimental import pallas as pl
from jax.experimental.pallas import tpu as pltpu
from jax.sharding import PartitionSpec as P

Z_HI = 3
ROOM = 48


def dot(a, b):
    return jnp.dot(a, b, preferred_element_type=jnp.float32)


def dot_t(a, b):
    return lax.dot_general(a, b, (((1,), (1,)), ((), ())), preferred_element_type=jnp.float32)


def onehot_of(asked, my_row, owned):
    rows, _, slots = asked.shape
    per_block = slots // rows
    shape = (rows * per_block, slots)
    spread = jnp.broadcast_to(asked[...], (rows, per_block, slots)).reshape(shape)
    wanted = my_row[0, 0] * per_block + lax.broadcasted_iota(jnp.int32, shape, 0) % per_block
    lane = lax.broadcasted_iota(jnp.int32, shape, 1)
    index = jnp.sum(jnp.where(wanted == lane, spread, 0), axis=1, keepdims=True)
    node = lax.broadcasted_iota(jnp.int32, (rows * per_block, owned), 1)
    return jnp.where(index % owned == node, 1.0, 0.0).astype(jnp.bfloat16)


def answer_kernel(asked, my_row, own, answer):
    answer[...] = dot(onehot_of(asked, my_row, own.shape[0]), own[...]).astype(jnp.bfloat16)


def column_of(row):
    n = row.shape[1]
    diagonal = lax.broadcasted_iota(jnp.int32, (n, n), 0) == lax.broadcasted_iota(jnp.int32, (n, n), 1)
    return jnp.sum(jnp.where(diagonal, row, 0), axis=1, keepdims=True)


def plan_kernel(height, nodes, cots, place, counts, own, note, target, rest):
    width = nodes.shape[1]
    slots = place.shape[1]
    per_block = slots // counts.shape[1]
    own[:, :width] = nodes[...]
    own[:, width:] = cots[...]
    expand = (
        lax.broadcasted_iota(jnp.int32, (counts.shape[1], slots), 0)
        == lax.broadcasted_iota(jnp.int32, (counts.shape[1], slots), 1) // per_block
    )
    block_counts = column_of(counts[...])
    count = jnp.sum(jnp.where(expand, block_counts, 0), axis=0, keepdims=True)
    alive = lax.broadcasted_iota(jnp.int32, (1, slots), 1) % per_block < count
    neighbour = jnp.where(alive, place[...] // height, -1)
    inside = place[...] % height
    earlier = lax.broadcasted_iota(jnp.int32, (slots, slots), 0) < lax.broadcasted_iota(
        jnp.int32, (slots, slots), 1
    )
    same = (column_of(neighbour) == neighbour) & earlier
    rank = jnp.sum(jnp.where(same, 1, 0), axis=0, keepdims=True)
    fits = alive & (rank < ROOM - 1)
    left = alive & (rank >= ROOM - 1)
    target[...] = jnp.where(fits, neighbour * ROOM + rank, -1)
    rest[...] = jnp.where(left, place[...], -1)
    over = jnp.max(jnp.where(left, 1.0, 0.0))
    shape = note.shape
    row = lax.broadcasted_iota(jnp.int32, (shape[0], slots), 0)
    told = (row % ROOM == ROOM - 1) & (row // ROOM == neighbour) & fits
    values = jnp.where(told, inside, 0).astype(jnp.float32).astype(jnp.bfloat16)
    at = lax.broadcasted_iota(jnp.int32, (width, slots), 0) == rank
    lines = dot_t(values, jnp.where(at, 1.0, 0.0).astype(jnp.bfloat16))
    flag = (lax.broadcasted_iota(jnp.int32, shape, 0) % ROOM == ROOM - 1) & (
        lax.broadcasted_iota(jnp.int32, shape, 1) == width - 1
    )
    note[...] = jnp.where(flag, over, lines).astype(jnp.bfloat16)


def edge_kernel(
    table, sender, target, note, recv, counts, w_out, vectors, edges, edge_cot, w_hbm,
    new_edges, packed, compact,
    w_in, sems,
):
    slots, width = edges.shape
    group = table.shape[0]
    per_block = slots // counts.shape[1]
    w_copies = [
        pltpu.make_async_copy(
            w_hbm.at[pl.ds(part * width, width), :], w_in.at[pl.ds(part * width, width), :], sems.at[part]
        )
        for part in range(3)
    ]
    for copy in (w_copies[1], w_copies[2], w_copies[0]):
        copy.start()
    b_in, b_out = vectors[0:1, :], vectors[1:2, :]
    gain, bias = vectors[2:3, :], vectors[3:4, :]
    pick = column_of(sender[...])
    slot = lax.broadcasted_iota(jnp.int32, (slots, counts.shape[1]), 0)
    block = lax.broadcasted_iota(jnp.int32, (slots, counts.shape[1]), 1)
    count = jnp.sum(jnp.where(slot // per_block == block, counts[...], 0), axis=1, keepdims=True)
    alive = slot[:, :1] % per_block < count
    lane = lax.broadcasted_iota(jnp.int32, (slots, group), 1)
    chosen = jnp.where(pick == lane, 1.0, 0.0).astype(jnp.bfloat16)
    send_feat = dot(chosen, table[...]).astype(jnp.bfloat16)
    cot = edge_cot[...].astype(jnp.float32) + recv[:, width:].astype(jnp.float32)
    scaled = jnp.where(alive, cot, 0.0) * gain
    scaled_mean = jnp.mean(scaled, axis=1, keepdims=True)
    row = lax.broadcasted_iota(jnp.int32, (compact.shape[0], slots), 0)
    returning = jnp.where(target[...] == row, 1.0, 0.0).astype(jnp.bfloat16)
    w_copies[1].wait()
    pre = dot(send_feat, w_in[width : 2 * width, :])
    w_copies[2].wait()
    pre += dot(recv[:, :width], w_in[2 * width :, :])
    w_copies[0].wait()
    pre += dot(edges[...], w_in[:width, :])
    pre += b_in
    sigma = jax.nn.sigmoid(pre)
    hidden = (pre * sigma).astype(jnp.bfloat16)
    outer = dot(hidden, w_out[...]) + b_out
    center = outer - jnp.mean(outer, axis=1, keepdims=True)
    inv_std = lax.rsqrt(jnp.mean(center * center, axis=1, keepdims=True) + 1e-05)
    normed = center * inv_std
    message = jnp.where(alive, normed * gain + bias, 0.0).astype(jnp.bfloat16)
    packed[:, :width] = message
    new_edges[...] = (edges[...].astype(jnp.float32) + message.astype(jnp.float32)).astype(jnp.bfloat16)
    d_outer = inv_std * (
        scaled
        - scaled_mean
        - normed * jnp.mean(scaled * normed, axis=1, keepdims=True)
    )
    d_hidden = dot_t(d_outer.astype(jnp.bfloat16), w_out[...])
    d_pre = (d_hidden * sigma * (1.0 + pre * (1.0 - sigma))).astype(jnp.bfloat16)
    packed[:, width:] = d_pre
    compact[...] = (dot(returning, d_pre) + note[...].astype(jnp.float32)).astype(jnp.bfloat16)


def dense_kernel(packed, place, partial):
    width = partial.shape[1]
    row = lax.broadcasted_iota(jnp.int32, (partial.shape[0], packed.shape[0]), 0)
    placed = jnp.where(place[...] == row, 1.0, 0.0).astype(jnp.bfloat16)
    partial[...] = dot(placed, packed[:, width:]).astype(jnp.bfloat16)


def place_kernel(arrived, column_sum, overflow):
    height, width = column_sum.shape
    row = lax.broadcasted_iota(jnp.int32, (height, ROOM), 0).astype(jnp.float32)
    data = lax.broadcasted_iota(jnp.int32, (height, ROOM), 1) < ROOM - 1
    last = lax.broadcasted_iota(jnp.int32, (16, width), 0) == 15
    total = jnp.zeros(column_sum.shape, jnp.float32)
    over = jnp.zeros((1, 128), jnp.float32)
    for at in range(0, arrived.shape[0], ROOM):
        note = arrived[at + ROOM - 16 : at + ROOM, :].astype(jnp.float32)
        line = jnp.sum(jnp.where(last, note, 0.0), axis=0, keepdims=True)
        placed = jnp.where((line[:, :ROOM] == row) & data, 1.0, 0.0).astype(jnp.bfloat16)
        total += dot(placed, arrived[at : at + ROOM, :])
        over = jnp.maximum(over, line[:, width - 128 :])
    column_sum[...] = total
    end = lax.broadcasted_iota(jnp.int32, over.shape, 1) == 127
    overflow[0, 0] = (jnp.max(jnp.where(end, over, 0.0)) > 0.5).astype(jnp.int32)


def owner_kernel(asked, my_row, returned, column_sum, to_below, to_above, w_in, aggregated, grad_nodes):
    owned, width = aggregated.shape
    onehot = onehot_of(asked, my_row, owned)
    summed = lax.dot_general(
        onehot, returned[...], (((0,), (0,)), ((), ())), preferred_element_type=jnp.float32
    )
    aggregated[...] = summed[:, :width].astype(jnp.bfloat16)
    sent = column_sum[:owned, :] + to_below[...].astype(jnp.float32) + to_above[...].astype(jnp.float32)
    grad = dot_t(sent.astype(jnp.bfloat16), w_in[width : 2 * width, :])
    grad += dot_t(summed[:, width:].astype(jnp.bfloat16), w_in[2 * width :, :])
    grad_nodes[...] = grad.astype(jnp.bfloat16)


VMEM = pl.BlockSpec(memory_space=pltpu.VMEM)
ANY = pl.BlockSpec(memory_space=pl.ANY)
SMEM = pl.BlockSpec(memory_space=pltpu.SMEM)


def on_device(
    node_latents,
    edge_latents,
    edge_sender,
    edge_receiver,
    edge_count,
    w_in,
    b_in,
    w_out,
    b_out,
    ln_gain,
    ln_bias,
    agg_cotangent,
    edge_cotangent,
):
    owned, width = node_latents.shape
    slots = edge_latents.shape[0]
    rows = lax.axis_size("row")
    cols = lax.axis_size("col")
    per_block = slots // rows
    tall = cols // Z_HI
    along_y = [[y * Z_HI + h for y in range(tall)] for h in range(Z_HI)]
    up = [(y * Z_HI + h, y * Z_HI + (h + 1) % Z_HI) for y in range(tall) for h in range(Z_HI)]
    down = [(b, a) for a, b in up]
    my_h = lax.axis_index("col") % Z_HI

    height = Z_HI * owned
    device = edge_sender // owned
    turn = (my_h - device % Z_HI + Z_HI) % Z_HI
    place = (device // Z_HI) * height + turn * owned + edge_sender % owned
    place = place.reshape(1, slots)
    own, note, target, rest = pl.pallas_call(
        functools.partial(plan_kernel, height),
        in_specs=[VMEM] * 4,
        out_specs=[VMEM] * 4,
        out_shape=[
            jax.ShapeDtypeStruct((owned, 2 * width), jnp.bfloat16),
            jax.ShapeDtypeStruct((tall * ROOM, width), jnp.bfloat16),
            jax.ShapeDtypeStruct((1, slots), jnp.int32),
            jax.ShapeDtypeStruct((1, slots), jnp.int32),
        ],
        cost_estimate=pl.CostEstimate(
            flops=2 * tall * ROOM * slots * width, bytes_accessed=256 * 1024, transcendentals=0
        ),
        compiler_params=pltpu.CompilerParams(vmem_limit_bytes=16 * 1024 * 1024),
    )(node_latents, agg_cotangent, place, edge_count)
    from_below = lax.ppermute(node_latents, "col", up)
    from_above = lax.ppermute(node_latents, "col", down)
    my_row = lax.axis_index("row").astype(jnp.int32).reshape(1, 1)
    indices = jnp.broadcast_to(edge_receiver.reshape(1, 1, slots), (rows, 1, slots))
    asked = lax.all_to_all(indices, "row", 0, 0, tiled=True)
    answer = pl.pallas_call(
        answer_kernel,
        in_specs=[VMEM, SMEM, VMEM],
        out_specs=VMEM,
        out_shape=jax.ShapeDtypeStruct((slots, 2 * width), jnp.bfloat16),
        cost_estimate=pl.CostEstimate(
            flops=4_000_000_000, bytes_accessed=640 * 1024, transcendentals=0
        ),
        compiler_params=pltpu.CompilerParams(vmem_limit_bytes=16 * 1024 * 1024),
    )(asked, my_row, own)
    answer, from_below, from_above = lax.optimization_barrier((answer, from_below, from_above))
    recv = lax.all_to_all(answer, "row", 0, 0, tiled=True)
    column = jnp.concatenate([node_latents, from_below, from_above], axis=0)
    table = lax.all_gather(column, "col", axis=0, tiled=True, axis_index_groups=along_y)

    vectors = jnp.stack([b_in, b_out, ln_gain, ln_bias])

    new_edges, packed, compact = pl.pallas_call(
        edge_kernel,
        in_specs=[VMEM] * 10 + [ANY],
        out_specs=[VMEM] * 3,
        out_shape=[
            jax.ShapeDtypeStruct((slots, width), jnp.bfloat16),
            jax.ShapeDtypeStruct((slots, 2 * width), jnp.bfloat16),
            jax.ShapeDtypeStruct((tall * ROOM, width), jnp.bfloat16),
        ],
        scratch_shapes=[
            pltpu.VMEM((3 * width, width), jnp.bfloat16),
            pltpu.SemaphoreType.DMA((3,)),
        ],
        compiler_params=pltpu.CompilerParams(vmem_limit_bytes=50 * 1024 * 1024),
        cost_estimate=pl.CostEstimate(
            flops=2 * slots * width * (5 * width + 2 * cols * owned),
            bytes_accessed=6 * 1024 * 1024,
            transcendentals=slots * width,
        ),
    )(
        table, place, target, note, recv, edge_count, w_out, vectors,
        edge_latents, edge_cotangent, w_in,
    )

    arrived = lax.all_to_all(compact, "col", 0, 0, tiled=True, axis_index_groups=along_y)
    column_sum, overflow = pl.pallas_call(
        place_kernel,
        in_specs=[VMEM],
        out_specs=[VMEM, SMEM],
        out_shape=[
            jax.ShapeDtypeStruct((height, width), jnp.float32),
            jax.ShapeDtypeStruct((1, 1), jnp.int32),
        ],
        compiler_params=pltpu.CompilerParams(vmem_limit_bytes=16 * 1024 * 1024),
    )(arrived)

    def with_rest():
        partial = pl.pallas_call(
            dense_kernel,
            in_specs=[VMEM] * 2,
            out_specs=VMEM,
            out_shape=jax.ShapeDtypeStruct((tall * height, width), jnp.bfloat16),
            compiler_params=pltpu.CompilerParams(vmem_limit_bytes=16 * 1024 * 1024),
        )(packed, rest)
        parts = lax.all_to_all(partial, "col", 0, 0, tiled=True, axis_index_groups=along_y)
        return column_sum + jnp.sum(parts.reshape(tall, height, width).astype(jnp.float32), axis=0)

    column_sum = lax.cond(overflow[0, 0] > 0, with_rest, lambda: column_sum)
    away = column_sum.astype(jnp.bfloat16)
    to_below = lax.ppermute(away[owned : 2 * owned], "col", down)
    to_above = lax.ppermute(away[2 * owned :], "col", up)

    returned = lax.all_to_all(packed, "row", 0, 0, tiled=True)
    aggregated, grad_nodes = pl.pallas_call(
        owner_kernel,
        in_specs=[VMEM, SMEM] + [VMEM] * 5,
        out_specs=[VMEM] * 2,
        out_shape=[jax.ShapeDtypeStruct((owned, width), jnp.bfloat16)] * 2,
        cost_estimate=pl.CostEstimate(
            flops=2 * owned * width * (2 * slots + 2 * width), bytes_accessed=2 * 1024 * 1024, transcendentals=0
        ),
        compiler_params=pltpu.CompilerParams(vmem_limit_bytes=16 * 1024 * 1024),
    )(asked, my_row, returned, column_sum, to_below, to_above, w_in)
    d_edge = dot_t(packed[:, width:], w_in[:width])
    grad_edges = (edge_cotangent.astype(jnp.float32) + d_edge).astype(jnp.bfloat16)
    return (new_edges, aggregated, grad_nodes, grad_edges)


def solution(mesh):
    split = P(("row", "col"), None)
    return jax.shard_map(
        on_device,
        mesh=mesh,
        in_specs=(
            split, split, P(("row", "col")), P(("row", "col")), split,
            P(), P(), P(), P(), P(), P(), split, split,
        ),
        out_specs=(split, split, split, split),
        check_vma=False,
    )
```
